128 devices in a mesh: expert: 32 (over y, x, core), dp: 4 (over z).
Axes of the slice: x: 4, y: 4, z: 4, core: 2. Of those that a mesh axis runs over, the one named last changes fastest.
Arguments:
- tokens: bfloat16 [16384, 7168], P(('expert', 'dp')), may hold values from -6 to 6
- routes: int32 [16384, 8], P(('expert', 'dp')), may hold values from 0 to 31, all different within a row; in each aligned block of 128 rows (0 to 127, 128 to 255, ...) at most 40 rows name the same one
- slab_start: int32 [32], replicated, may hold values from 0 to 6720, as said below
Outputs:
- gram_slab: float32 [32, 448, 7168], P('expert', None, 'dp')
The draws below stay inside these ranges and needn't reach their ends.
Inputs may be any that keep to these rules, and one draw needn't show every extreme that they name: `routes`: within the rows of one device no expert is named by more than 40 rows, a bound that some block reaches of them; every expert is named somewhere. `slab_start`: multiples of 8.
All inputs are finite; a program needn't handle non-finite values.
Results may differ from the reference program's by a relative error of at most 0.0003.
Values may be sent and summed in bfloat16 or wider, within the bound.
A program may use at most 256 MiB of HBM per device.

```python
import math
import jax
import jax.numpy as jnp
import numpy as np
from jax import lax

D = 7168
TOP = 8
SLAB = 448
EXPERTS = 32
TOK_DEV = 128
CAP = 40
TOKENS = 16384
N_EXPERT = 32
N_DP = 4


def draw_slab_start(key, part):
    key = jax.random.fold_in(key, 7)
    steps = jax.random.randint(key, (EXPERTS,), 0, (D - SLAB) // 8 + 1)
    return (steps * 8).astype(jnp.int32)


def steps_of(rng, extent, cuts, least, top_value):
    factor_of = 1.0
    for position, parts in cuts:
        steps = jax.random.uniform(jax.random.fold_in(jax.random.fold_in(rng, 6), position), (parts,), jnp.float32, least / len(cuts), top_value / len(cuts))
        factor_of = factor_of * jnp.repeat(jnp.exp(steps), extent[position] // parts).reshape((-1,) + (1,) * (len(extent) - 1 - position))
    return factor_of


def deal_out(stream_key, own, number, rows, number_of, top, bound, slope):
    sequence = jax.random.permutation(stream_key, number_of)
    heavy_load, usual = shares(number_of, rows * top, bound, slope, True), shares(number_of, rows * top, bound, slope, False)
    places = jnp.arange(number_of)

    def named(lengths, rotation):
        used = int((lengths > 0).sum())
        fixed = max(1, used // 4)
        shifted = fixed + (places - fixed + rotation * (used - fixed)) % max(1, number_of - fixed)
        return jnp.zeros((number_of,), jnp.int32).at[sequence[jnp.where(places < fixed, places, shifted)]].set(jnp.asarray(lengths, jnp.int32))

    lengths = jnp.where(number % 4 == 0, named(heavy_load, number // 4), named(usual, number - number // 4 - 1))
    mixed = jax.random.permutation(jax.random.fold_in(own, 3), number_of)
    donor, sink = mixed[0:number_of // 2 * 2:2], mixed[1:number_of // 2 * 2:2]
    room = jnp.minimum(lengths[donor] - 1, bound - lengths[sink]) // 2
    room = jnp.where((donor == sequence[0]) | (sink == sequence[0]) | (lengths[sink] == 0), 0, jnp.maximum(room, 0))
    shifted = jax.random.randint(jax.random.fold_in(own, 4), (number_of // 2,), 0, 1 << 20) % (room + 1)
    lengths = lengths.at[donor].add(-shifted).at[sink].add(shifted)
    labels = jnp.searchsorted(jnp.cumsum(lengths), jnp.arange(rows * top), side="right").astype(jnp.int32)
    listing = labels.reshape(top, rows).T
    listing = listing[jax.random.permutation(jax.random.fold_in(own, 1), rows)]
    rotation = jax.random.randint(jax.random.fold_in(own, 2), (rows, 1), 0, top)
    return jnp.take_along_axis(listing, (jnp.arange(top)[None, :] + rotation) % top, axis=1)


def shares(number_of, total, bound, slope, full):
    loads = [(1 << 20) // math.isqrt(grade ** slope) + 1 for grade in range(1, number_of + 1)]
    largest = bound if full else min(bound, max(-(-total // number_of), total * loads[0] // sum(loads)))
    least = 1 if total - largest >= number_of - 1 else 0
    given, surplus = [largest] + [least] * (number_of - 1), total - largest - least * (number_of - 1)
    while surplus > 0:
        movable = [i for i in range(1, number_of) if given[i] < largest] or [i for i in range(1, number_of) if given[i] < bound]
        pool, budget = sum([loads[i] for i in movable]), surplus
        for i in movable:
            addition = min(bound - given[i], max(1, budget * loads[i] // pool), surplus)
            given[i] = given[i] + addition
            surplus = surplus - addition
    return np.array(given)


def noise(rng, dims, spread, limit, cuts=(), kind=jnp.bfloat16):
    drawn = spread * jax.random.normal(rng, dims, jnp.float32)
    if cuts:
        drawn = drawn * steps_of(rng, dims, cuts, -0.22, 0.18)
    return jnp.clip(drawn, -limit, limit).astype(kind)


def setup_inputs(seed: int = 0) -> dict:
    splits = jax.random.split(jax.random.key(seed), 4)
    tokens = noise(splits[0], (TOKENS, D), 1.0, 6.0, ((0, 128),))
    routes_keys = jax.random.split(jax.random.fold_in(splits[1], 1), TOKENS // TOK_DEV)
    routes_turns = jax.random.permutation(jax.random.fold_in(splits[1], 3), TOKENS // TOK_DEV)
    routes = jax.vmap(lambda own, number: deal_out(jax.random.fold_in(splits[1], 2), own, number, TOK_DEV, EXPERTS, TOP, CAP, 1))(routes_keys, routes_turns).reshape((TOKENS, TOP))
    slab_start = draw_slab_start(jax.random.fold_in(splits[3], 71), 0)
    return dict(tokens=tokens, routes=routes, slab_start=slab_start)


def reference(tokens, routes, slab_start):
    row_limit = min(TOKENS, N_EXPERT * N_DP * CAP)

    def one_expert(expert):
        hit = jnp.any(routes == expert, axis=1)
        order = jnp.argsort(jnp.where(hit, 0, 1).astype(jnp.int32), stable=True)[:row_limit]
        keep = hit[order].astype(jnp.float32)
        routed = tokens[order].astype(jnp.float32) * keep[:, None]
        start = lax.dynamic_index_in_dim(slab_start, expert, keepdims=False).astype(jnp.int32)
        window = lax.dynamic_slice_in_dim(routed, start, SLAB, 1)
        gram = jnp.dot(window.T, routed, preferred_element_type=jnp.float32)
        return gram / jnp.sum(hit.astype(jnp.float32))

    return lax.map(one_expert, jnp.arange(EXPERTS, dtype=jnp.int32))
```

```python
import functools

import jax
import jax.numpy as jnp
from jax import lax
from jax.experimental import pallas as pl
from jax.experimental.pallas import tpu as pltpu
from jax.sharding import PartitionSpec as P

MESH = pl.DeviceIdType.MESH
SLAB = 448
CAP = 40
PAIR = 2 * CAP
WIDE = 512
RING = 4
TOK = 128
WIDTH = 7168
BLOCK = WIDTH // RING
CHUNK = 256
CHUNKS = BLOCK // CHUNK
ROWS = RING * RING * 2 * TOK
GROUPS = 4
OFFSETS = (2, 1, 3, 0)
SCALE_ROWS = 112
HALF = SLAB // 2
SPAN = 640

ORDER = ("P", "XB", "XA", "Z", "WZ", "WZF", "C", "EXP", "U")
SCHEDULE = (
    "XA0", "P0", "XA1", "P1", "P2", "WZ0", "XB0", "XA2", "Z3", "P3", "WZ1", "WZF0", "C0", "XB1", "XA3", "Z4", "WZ2",
    "EXP0", "U00", "WZF1", "C1", "XB2", "XA4", "Z5", "WZ3", "EXP1", "U01", "U10", "U11", "WZF2", "C2", "XB3", "XA5",
    "Z6", "EXP2", "U02", "U12", "U20", "U21", "U22", "WZF3", "C3", "XB4", "XA6", "U03", "U13", "U23", "EXP3", "U30",
    "C4", "XB5", "U04", "U14", "U24", "U31", "C5", "XB6", "U05", "U15", "U25", "U32", "C6", "U06", "U16", "U26",
    "U33", "U34", "U35", "U36",
)


def plan():
    tables = {name: {} for name in ORDER}
    step, last = 0, -1
    for item in SCHEDULE:
        name = item.rstrip("0123456789")
        digits = item[len(name):]
        value = int(digits[0]) * CHUNKS + int(digits[1]) if name == "U" else int(digits)
        rank = ORDER.index(name)
        if rank <= last:
            step += 1
        last = rank
        tables[name][step] = value
    return tables, step + 1


def looked_up(table, step):
    value = jnp.int32(-1)
    for at, entry in table.items():
        value = jnp.where(step == at, jnp.int32(entry), value)
    return value


def offset_of(group):
    value = jnp.int32(OFFSETS[0])
    for index in range(1, GROUPS):
        value = jnp.where(group == index, jnp.int32(OFFSETS[index]), value)
    return value


def gram_kernel(
    start_ref, routes_ref, tok_ref, out_ref,
    both, listed, slots, packed, win, wide, cols, part, quant, scale, half_q, half_s, full_q, full_s, hits,
    pair_s, pair_r, own_s, z_s, z_r, zl_s, xa_s, xa_r, xb_s, xb_r, c_s, c_r,
    wx_s, wx_r, wz_s, wz_r, wf_s, wf_r, hq_s, hq_r, hs_s, hs_r, fq_s, fq_r, fs_s, fs_r,
):
    expert = lax.axis_index("expert")
    z = lax.axis_index("dp")
    core = expert % 2
    x = (expert // 2) % RING
    y = expert // (2 * RING)

    def device(dy=0, dx=0, dz=0, dc=0):
        ey, ex, ec = (y + dy) % RING, (x + dx) % RING, (core + dc) % 2
        return ((ey * RING + ex) * 2 + ec, (z + dz) % RING)

    def remote(src, dst, send, recv, to):
        return pltpu.make_async_remote_copy(
            src_ref=src, dst_ref=dst, send_sem=send, recv_sem=recv, device_id=to, device_id_type=MESH
        )

    def pair_copies():
        return (
            remote(routes_ref, listed.at[core], pair_s.at[0], pair_r.at[0], device(dc=1)),
            remote(tok_ref, both.at[pl.ds(core * TOK, TOK)], pair_s.at[1], pair_r.at[1], device(dc=1)),
        )

    def own_copy():
        return pltpu.make_async_copy(tok_ref, both.at[pl.ds(core * TOK, TOK)], own_s)

    def z_copy(k, d):
        first = pl.multiple_of(((z + d) % RING) * BLOCK + k * CHUNK, 128)
        return remote(
            tok_ref.at[:, pl.ds(first, CHUNK)], cols.at[k, core, x, z], z_s.at[k, d - 1], z_r.at[k, d - 1], device(dz=d)
        )

    def z_local(k):
        first = pl.multiple_of(z * BLOCK + k * CHUNK, 128)
        return pltpu.make_async_copy(tok_ref.at[:, pl.ds(first, CHUNK)], cols.at[k, core, x, z], zl_s.at[k])

    def xa_copy(k, way):
        here = cols.at[k, core, x]
        return remote(here, here, xa_s.at[k, way], xa_r.at[k, way], device(dx=1 if way == 0 else 3))

    def xb_copy(k, way):
        origin = (x + (3 if way == 0 else 1)) % RING
        here = cols.at[k, core, origin, pl.ds(2 * way, 2)]
        return remote(here, here, xb_s.at[k, way], xb_r.at[k, way], device(dx=1 if way == 0 else 3))

    def c_copy(k):
        here = cols.at[k, core]
        return remote(here, here, c_s.at[k], c_r.at[k], device(dc=1))

    def wx_copy(g, d):
        return remote(
            packed.at[g * RING + d], win.at[g, z, x], wx_s.at[g, d - 1], wx_r.at[g, d - 1], device(dx=d)
        )

    def wz_copy(g, way):
        here = win.at[g, z]
        return remote(here, here, wz_s.at[g, way], wz_r.at[g, way], device(dz=1 if way == 0 else 3))

    def wf_copy(g, way):
        origin = (z + (3 if way == 0 else 1)) % RING
        here = win.at[g, origin, pl.ds(2 * way, 2)]
        return remote(here, here, wf_s.at[g, way], wf_r.at[g, way], device(dz=1 if way == 0 else 3))

    def half_copies(k, way):
        to = device(dy=1 if way == 0 else 3)
        return (
            remote(quant.at[0, k, pl.ds(way * HALF, HALF)], half_q.at[way, k], hq_s.at[way, k], hq_r.at[way, k], to),
            remote(scale.at[0, k], half_s.at[way, k], hs_s.at[way, k], hs_r.at[way, k], to),
        )

    def full_copies(g, k):
        way = g - 1
        to = device(dy=jnp.where(g == 1, 1, 3))
        return (
            remote(quant.at[g, k], full_q.at[way, k], fq_s.at[way, k], fq_r.at[way, k], to),
            remote(scale.at[g, k], full_s.at[way, k], fs_s.at[way, k], fs_r.at[way, k], to),
        )

    barrier = pltpu.get_barrier_semaphore()
    peers = [device(dc=1), device(dy=1), device(dy=3)]
    peers += [device(dx=d) for d in (1, 2, 3)] + [device(dz=d) for d in (1, 2, 3)]
    for peer in peers:
        pl.semaphore_signal(barrier, inc=1, device_id=peer, device_id_type=MESH)
    pl.semaphore_wait(barrier, len(peers))

    def send_z(k):
        for d in (1, 3, 2):
            z_copy(k, d).start()
        z_local(k).start()

    for copy in pair_copies():
        copy.start()
    own_copy().start()
    for k in range(3):
        send_z(jnp.int32(k))
    listed[core] = routes_ref[...]

    def take_xa(k):
        for d in (1, 2, 3):
            z_copy(k, d).wait_recv()
        z_local(k).wait()
        for way in (0, 1):
            xa_copy(k, way).start()

    def take_xb(k):
        for way in (0, 1):
            xa_copy(k, way).wait_recv()
            xb_copy(k, way).start()

    def take_c(k):
        for way in (0, 1):
            xb_copy(k, way).wait_recv()
        c_copy(k).start()

    def find_slots():
        for copy in pair_copies():
            copy.wait_recv()
        own_copy().wait()
        named = jnp.concatenate([listed[0], listed[1]], axis=1)
        row = lax.broadcasted_iota(jnp.int32, (GROUPS * RING, 2 * TOK), 0)
        group, step = row // RING, row % RING
        away = jnp.where(group == 0, OFFSETS[0], jnp.where(group == 1, OFFSETS[1], jnp.where(group == 2, OFFSETS[2], OFFSETS[3])))
        label = (((y + away) % RING) * RING + (x + step) % RING) * 2 + core
        hit = jnp.zeros((GROUPS * RING, 2 * TOK), jnp.float32)
        for choice in range(named.shape[0]):
            hit += jnp.where(named[choice:choice + 1, :] == label, 1.0, 0.0)
        before = lax.broadcasted_iota(jnp.int32, (2 * TOK, 2 * TOK), 0) < lax.broadcasted_iota(
            jnp.int32, (2 * TOK, 2 * TOK), 1
        )
        rank = jnp.dot(
            hit.astype(jnp.bfloat16), jnp.where(before, 1.0, 0.0).astype(jnp.bfloat16), preferred_element_type=jnp.float32
        )
        slots[...] = jnp.where(hit > 0.0, rank, -1.0)

    def take_p(g):
        pl.when(g == 0)(find_slots)
        slot = lax.broadcasted_iota(jnp.int32, (PAIR, 2 * TOK), 0).astype(jnp.float32)
        number = (lax.broadcasted_iota(jnp.int32, (2 * TOK, 128), 0) + 1).astype(jnp.float32).astype(jnp.bfloat16)
        lane = lax.broadcasted_iota(jnp.int32, (PAIR, 128), 1)
        source = lax.broadcasted_iota(jnp.int32, (SPAN, WIDE), 0)
        target = lax.broadcasted_iota(jnp.int32, (SPAN, WIDE), 1)
        for d in (2, 1, 3, 0):
            row = g * RING + d
            chosen = jnp.where(slots[pl.ds(row, 1), :] == slot, 1.0, 0.0).astype(jnp.bfloat16)
            label = (((y + offset_of(g)) % RING) * RING + (x + d) % RING) * 2 + core
            start = start_ref[label]
            tile = jnp.minimum(lax.div(start, jnp.int32(128)), (WIDTH - SPAN) // 128)
            shift = start - tile * 128
            first = tile * 128
            rows = both[:, pl.ds(first, SPAN)]
            picked = jnp.dot(chosen, rows, preferred_element_type=jnp.float32)
            moved = jnp.where(source == target + shift, 1.0, 0.0).astype(jnp.bfloat16)
            picked = jnp.dot(picked.astype(jnp.bfloat16), moved, preferred_element_type=jnp.float32)
            index = jnp.dot(chosen, number, preferred_element_type=jnp.float32)
            last = jnp.where(lane >= SLAB - 384, index, picked[:, 384:512])
            value = jnp.concatenate([picked[:, :384], last], axis=1).astype(jnp.bfloat16)
            if d == 0:
                win[g, z, x] = value
            else:
                packed[row] = value
                wx_copy(g, d).start()

    def take_wz(g):
        for d in (1, 2, 3):
            wx_copy(g, d).wait_recv()
        for way in (0, 1):
            wz_copy(g, way).start()

    def take_wzf(g):
        for way in (0, 1):
            wz_copy(g, way).wait_recv()
            wf_copy(g, way).start()

    def take_exp(g):
        for way in (0, 1):
            wf_copy(g, way).wait_recv()
        token = (lax.broadcasted_iota(jnp.int32, (PAIR, 2 * TOK), 1) + 1).astype(jnp.float32)

        def one(place, total):
            held = win[g, place % RING, place // RING]
            index = held[:, SLAB:SLAB + 1].astype(jnp.float32)
            chosen = jnp.where(index == token, 1.0, 0.0)
            full = lax.dot_general(
                held[:, :SLAB], chosen.astype(jnp.bfloat16), (((0,), (0,)), ((), ())), preferred_element_type=jnp.float32
            ).astype(jnp.bfloat16)
            for side in (0, 1):
                at = pl.multiple_of((side * RING * RING + place) * TOK, 128)
                wide[g, :, pl.ds(at, TOK)] = full[:, side * TOK:(side + 1) * TOK]
            return total + jnp.sum(chosen, axis=0, keepdims=True)

        hits[g] = lax.fori_loop(0, RING * RING, one, jnp.zeros((1, 2 * TOK), jnp.float32))

    def restored(block_q, row_scale):
        return block_q.astype(jnp.int32).astype(jnp.float32) * row_scale

    def take_u(unit):
        g, k = unit // CHUNKS, unit % CHUNKS

        @pl.when(g == 0)
        def _():
            c_copy(k).wait_recv()

        tokens = cols[k].reshape(ROWS, CHUNK)
        part[...] = jnp.dot(wide[g], tokens, preferred_element_type=jnp.float32)

        @pl.when(g == 3)
        def _():
            out_ref[:, pl.ds(pl.multiple_of(k * CHUNK, 128), CHUNK)] = part[...]

        @pl.when(g < 3)
        def _():
            scale[g, k, pl.ds(7, 1), :] = hits[g]

        for way in (0, 1):
            @pl.when(g == 1 + way)
            def _():
                for copy in half_copies(k, way):
                    copy.wait_recv()
                for piece in range(2):
                    rows = pl.ds(way * HALF + piece * SCALE_ROWS, SCALE_ROWS)
                    part[rows, :] += restored(
                        half_q[way, k, pl.ds(piece * SCALE_ROWS, SCALE_ROWS), :],
                        half_s[way, k, pl.ds(2 * way + piece, 1), :],
                    )
                if way == 0:
                    scale[g, k, pl.ds(7, 1), :] = hits[g] + half_s[way, k, pl.ds(7, 1), :]

        @pl.when(g < 3)
        def _():
            for piece in range(SLAB // SCALE_ROWS):
                rows = pl.ds(piece * SCALE_ROWS, SCALE_ROWS)
                block = part[rows, :]
                most = jnp.max(jnp.abs(block), axis=0, keepdims=True)
                factor = jnp.where(most > 0.0, 32767.0 / jnp.where(most > 0.0, most, 1.0), 0.0)
                quant[g, k, rows, :] = jnp.round(block * factor).astype(jnp.int32).astype(jnp.int16)
                scale[g, k, pl.ds(piece, 1), :] = most * (1.0 / 32767.0)

        @pl.when(g == 0)
        def _():
            for way in (0, 1):
                for copy in half_copies(k, way):
                    copy.start()

        @pl.when((g == 1) | (g == 2))
        def _():
            for copy in full_copies(g, k):
                copy.start()

    actions = {
        "P": take_p, "XB": take_xb, "XA": take_xa, "Z": send_z, "WZ": take_wz, "WZF": take_wzf, "C": take_c,
        "EXP": take_exp, "U": take_u,
    }
    tables, steps = plan()

    def one_step(step, carry):
        for name in ORDER:
            value = looked_up(tables[name], step)
            pl.when(value >= 0)(functools.partial(actions[name], value))
        return carry

    lax.fori_loop(0, steps, one_step, 0)

    def finish(k, carry):
        for g in (1, 2):
            for copy in full_copies(jnp.int32(g), k):
                copy.wait_recv()
        count = hits[3] + full_s[0, k, pl.ds(7, 1), :] + full_s[1, k, pl.ds(7, 1), :]
        inverse = 1.0 / jnp.sum(count, axis=1, keepdims=True)
        at = pl.ds(pl.multiple_of(k * CHUNK, 128), CHUNK)
        for piece in range(SLAB // SCALE_ROWS):
            rows = pl.ds(piece * SCALE_ROWS, SCALE_ROWS)
            total = out_ref[rows, at]
            for way in (0, 1):
                total += restored(full_q[way, k, rows, :], full_s[way, k, pl.ds(piece, 1), :])
            out_ref[rows, at] = total * inverse
        return carry

    lax.fori_loop(0, CHUNKS, finish, 0)

    for copy in pair_copies():
        copy.wait_send()

    def drain(k, carry):
        for d in (1, 2, 3):
            z_copy(k, d).wait_send()
        for way in (0, 1):
            xa_copy(k, way).wait_send()
            xb_copy(k, way).wait_send()
            for copy in half_copies(k, way):
                copy.wait_send()
        c_copy(k).wait_send()
        for g in (1, 2):
            for copy in full_copies(jnp.int32(g), k):
                copy.wait_send()
        return carry

    lax.fori_loop(0, CHUNKS, drain, 0)

    def drain_windows(g, carry):
        for d in (1, 2, 3):
            wx_copy(g, d).wait_send()
        for way in (0, 1):
            wz_copy(g, way).wait_send()
            wf_copy(g, way).wait_send()
        return carry

    lax.fori_loop(0, GROUPS, drain_windows, 0)


def shards(tokens, routes, slab_start):
    dma = pltpu.SemaphoreType.DMA
    bf16, f32, i16 = jnp.bfloat16, jnp.float32, jnp.int16
    pairs = [(CHUNKS, 2)] * 2
    result = pl.pallas_call(
        gram_kernel,
        out_shape=jax.ShapeDtypeStruct((SLAB, BLOCK), f32),
        in_specs=[
            pl.BlockSpec(memory_space=pltpu.SMEM),
            pl.BlockSpec(memory_space=pltpu.VMEM),
            pl.BlockSpec(memory_space=pl.ANY),
        ],
        out_specs=pl.BlockSpec(memory_space=pltpu.VMEM),
        scratch_shapes=[
            pltpu.VMEM((2 * TOK, WIDTH), bf16),
            pltpu.VMEM((2, 8, TOK), jnp.int32),
            pltpu.VMEM((GROUPS * RING, 2 * TOK), f32),
            pltpu.VMEM((GROUPS * RING, PAIR, WIDE), bf16),
            pltpu.VMEM((GROUPS, RING, RING, PAIR, WIDE), bf16),
            pltpu.VMEM((GROUPS, SLAB, ROWS), bf16),
            pltpu.VMEM((CHUNKS, 2, RING, RING, TOK, CHUNK), bf16),
            pltpu.VMEM((SLAB, CHUNK), f32),
            pltpu.VMEM((3, CHUNKS, SLAB, CHUNK), i16),
            pltpu.VMEM((3, CHUNKS, 8, CHUNK), f32),
            pltpu.VMEM((2, CHUNKS, HALF, CHUNK), i16),
            pltpu.VMEM((2, CHUNKS, 8, CHUNK), f32),
            pltpu.VMEM((2, CHUNKS, SLAB, CHUNK), i16),
            pltpu.VMEM((2, CHUNKS, 8, CHUNK), f32),
            pltpu.VMEM((GROUPS, 1, 2 * TOK), f32),
            dma((2,)), dma((2,)), dma(()),
            dma((CHUNKS, 3)), dma((CHUNKS, 3)), dma((CHUNKS,)),
            dma((CHUNKS, 2)), dma((CHUNKS, 2)), dma((CHUNKS, 2)), dma((CHUNKS, 2)), dma((CHUNKS,)), dma((CHUNKS,)),
            dma((GROUPS, 3)), dma((GROUPS, 3)), dma((GROUPS, 2)), dma((GROUPS, 2)), dma((GROUPS, 2)), dma((GROUPS, 2)),
            dma((2, CHUNKS)), dma((2, CHUNKS)), dma((2, CHUNKS)), dma((2, CHUNKS)),
            dma((2, CHUNKS)), dma((2, CHUNKS)), dma((2, CHUNKS)), dma((2, CHUNKS)),
        ],
        compiler_params=pltpu.CompilerParams(
            collective_id=0, has_side_effects=True, vmem_limit_bytes=62 * 2**20
        ),
        name="gram",
    )(slab_start, routes.T, tokens)
    return result[None]


def solution(mesh):
    placed = (P(("expert", "dp"), None), P(("expert", "dp"), None), P())
    return jax.shard_map(
        shards, mesh=mesh, in_specs=placed, out_specs=P("expert", None, "dp"), check_vma=False
    )
```

```python
import functools

import jax
import jax.numpy as jnp
from jax import lax
from jax.experimental import pallas as pl
from jax.experimental.pallas import tpu as pltpu
from jax.sharding import PartitionSpec as P

MESH = pl.DeviceIdType.MESH
SLAB = 448
CAP = 40
PAIR = 2 * CAP
WIDE = 512
RING = 4
TOK = 128
WIDTH = 7168
BLOCK = WIDTH // RING
CHUNK = 256
CHUNKS = BLOCK // CHUNK
ROWS = RING * RING * 2 * TOK
GROUPS = 4
OFFSETS = (2, 1, 3, 0)
SCALE_ROWS = 112
HALF = SLAB // 2
SPAN = 640

ORDER = ("S", "P", "XB", "XA", "Z", "WZ", "WZF", "C", "EXP", "U")
SCHEDULE = (
    "XA0", "Z4", "S0", "P2", "Z6", "P0", "P1", "WZ2", "XA1", "XA4", "WZ0", "XB0", "WZF2", "XB1", "WZF0", "WZ1",
    "XB4", "XA6", "P3", "C0", "EXP2", "C1", "Z3", "EXP0", "C4", "U01", "WZF1", "U00", "U04", "Z5", "XB6", "XA3",
    "U21", "EXP1", "U10", "U24", "C6", "XA5", "U11", "U06", "WZ3", "XB3", "U20", "XB5", "XA2", "U14", "C3", "U26",
    "WZF3", "U03", "C5", "U16", "XB2", "U05", "U13", "U23", "C2", "EXP3", "U30", "U02", "U15", "U33", "U25", "U22",
    "U35", "U12", "U36", "U34", "U31", "U32",
)


def plan():
    tables = {name: {} for name in ORDER}
    step, last = 0, -1
    for item in SCHEDULE:
        name = item.rstrip("0123456789")
        digits = item[len(name):]
        value = int(digits[0]) * CHUNKS + int(digits[1]) if name == "U" else int(digits)
        rank = ORDER.index(name)
        if rank <= last:
            step += 1
        last = rank
        tables[name][step] = value
    return tables, step + 1


def looked_up(table, step):
    value = jnp.int32(-1)
    for at, entry in table.items():
        value = jnp.where(step == at, jnp.int32(entry), value)
    return value


def offset_of(group):
    value = jnp.int32(OFFSETS[0])
    for index in range(1, GROUPS):
        value = jnp.where(group == index, jnp.int32(OFFSETS[index]), value)
    return value


def gram_kernel(
    start_ref, routes_ref, tok_ref, out_ref,
    both, listed, slots, packed, win, wide, cols, part, quant, scale, half_q, half_s, full_q, full_s, hits,
    pair_s, pair_r, own_s, z_s, z_r, zl_s, xa_s, xa_r, xb_s, xb_r, c_s, c_r,
    wx_s, wx_r, wz_s, wz_r, wf_s, wf_r, hq_s, hq_r, hs_s, hs_r, fq_s, fq_r, fs_s, fs_r,
):
    expert = lax.axis_index("expert")
    z = lax.axis_index("dp")
    core = expert % 2
    x = (expert // 2) % RING
    y = expert // (2 * RING)

    def device(dy=0, dx=0, dz=0, dc=0):
        ey, ex, ec = (y + dy) % RING, (x + dx) % RING, (core + dc) % 2
        return ((ey * RING + ex) * 2 + ec, (z + dz) % RING)

    def remote(src, dst, send, recv, to):
        return pltpu.make_async_remote_copy(
            src_ref=src, dst_ref=dst, send_sem=send, recv_sem=recv, device_id=to, device_id_type=MESH
        )

    def pair_copies():
        return (
            remote(routes_ref, listed.at[core], pair_s.at[0], pair_r.at[0], device(dc=1)),
            remote(tok_ref, both.at[pl.ds(core * TOK, TOK)], pair_s.at[1], pair_r.at[1], device(dc=1)),
        )

    def own_copy():
        return pltpu.make_async_copy(tok_ref, both.at[pl.ds(core * TOK, TOK)], own_s)

    def z_copy(k, d):
        first = pl.multiple_of(((z + d) % RING) * BLOCK + k * CHUNK, 128)
        return remote(
            tok_ref.at[:, pl.ds(first, CHUNK)], cols.at[k, core, x, z], z_s.at[k, d - 1], z_r.at[k, d - 1], device(dz=d)
        )

    def z_local(k):
        first = pl.multiple_of(z * BLOCK + k * CHUNK, 128)
        return pltpu.make_async_copy(tok_ref.at[:, pl.ds(first, CHUNK)], cols.at[k, core, x, z], zl_s.at[k])

    def xa_copy(k, way):
        here = cols.at[k, core, x]
        return remote(here, here, xa_s.at[k, way], xa_r.at[k, way], device(dx=1 if way == 0 else 3))

    def xb_copy(k, way):
        origin = (x + (3 if way == 0 else 1)) % RING
        here = cols.at[k, core, origin, pl.ds(2 * way, 2)]
        return remote(here, here, xb_s.at[k, way], xb_r.at[k, way], device(dx=1 if way == 0 else 3))

    def c_copy(k):
        here = cols.at[k, core]
        return remote(here, here, c_s.at[k], c_r.at[k], device(dc=1))

    def wx_copy(g, d):
        return remote(
            packed.at[g * RING + d], win.at[g, z, x], wx_s.at[g, d - 1], wx_r.at[g, d - 1], device(dx=d)
        )

    def wz_copy(g, way):
        here = win.at[g, z]
        return remote(here, here, wz_s.at[g, way], wz_r.at[g, way], device(dz=1 if way == 0 else 3))

    def wf_copy(g, way):
        origin = (z + (3 if way == 0 else 1)) % RING
        here = win.at[g, origin, pl.ds(2 * way, 2)]
        return remote(here, here, wf_s.at[g, way], wf_r.at[g, way], device(dz=1 if way == 0 else 3))

    def half_copies(k, way):
        to = device(dy=1 if way == 0 else 3)
        return (
            remote(quant.at[0, k, pl.ds(way * HALF, HALF)], half_q.at[way, k], hq_s.at[way, k], hq_r.at[way, k], to),
            remote(scale.at[0, k], half_s.at[way, k], hs_s.at[way, k], hs_r.at[way, k], to),
        )

    def full_copies(g, k):
        way = g - 1
        to = device(dy=jnp.where(g == 1, 1, 3))
        return (
            remote(quant.at[g, k], full_q.at[way, k], fq_s.at[way, k], fq_r.at[way, k], to),
            remote(scale.at[g, k], full_s.at[way, k], fs_s.at[way, k], fs_r.at[way, k], to),
        )

    barrier = pltpu.get_barrier_semaphore()
    peers = [device(dc=1), device(dy=1), device(dy=3)]
    peers += [device(dx=d) for d in (1, 2, 3)] + [device(dz=d) for d in (1, 2, 3)]
    for peer in peers:
        pl.semaphore_signal(barrier, inc=1, device_id=peer, device_id_type=MESH)
    pl.semaphore_wait(barrier, len(peers))

    def send_z(k):
        for d in (1, 3, 2):
            z_copy(k, d).start()
        z_local(k).start()

    for copy in pair_copies():
        copy.start()
    own_copy().start()
    for k in range(3):
        send_z(jnp.int32(k))
    listed[core] = routes_ref[...]

    def take_xa(k):
        for d in (1, 2, 3):
            z_copy(k, d).wait_recv()
        z_local(k).wait()
        for way in (0, 1):
            xa_copy(k, way).start()

    def take_xb(k):
        for way in (0, 1):
            xa_copy(k, way).wait_recv()
            xb_copy(k, way).start()

    def take_c(k):
        for way in (0, 1):
            xb_copy(k, way).wait_recv()
        c_copy(k).start()

    def find_slots(_):
        for copy in pair_copies():
            copy.wait_recv()
        own_copy().wait()
        named = jnp.concatenate([listed[0], listed[1]], axis=1)
        row = lax.broadcasted_iota(jnp.int32, (GROUPS * RING, 2 * TOK), 0)
        group, step = row // RING, row % RING
        away = jnp.where(group == 0, OFFSETS[0], jnp.where(group == 1, OFFSETS[1], jnp.where(group == 2, OFFSETS[2], OFFSETS[3])))
        label = (((y + away) % RING) * RING + (x + step) % RING) * 2 + core
        hit = jnp.zeros((GROUPS * RING, 2 * TOK), jnp.float32)
        for choice in range(named.shape[0]):
            hit += jnp.where(named[choice:choice + 1, :] == label, 1.0, 0.0)
        before = lax.broadcasted_iota(jnp.int32, (2 * TOK, 2 * TOK), 0) < lax.broadcasted_iota(
            jnp.int32, (2 * TOK, 2 * TOK), 1
        )
        rank = jnp.dot(
            hit.astype(jnp.bfloat16), jnp.where(before, 1.0, 0.0).astype(jnp.bfloat16), preferred_element_type=jnp.float32
        )
        slots[...] = jnp.where(hit > 0.0, rank, -1.0)

    def take_p(g):
        slot = lax.broadcasted_iota(jnp.int32, (PAIR, 2 * TOK), 0).astype(jnp.float32)
        number = (lax.broadcasted_iota(jnp.int32, (2 * TOK, 128), 0) + 1).astype(jnp.float32).astype(jnp.bfloat16)
        lane = lax.broadcasted_iota(jnp.int32, (PAIR, 128), 1)
        source = lax.broadcasted_iota(jnp.int32, (SPAN, WIDE), 0)
        target = lax.broadcasted_iota(jnp.int32, (SPAN, WIDE), 1)
        for d in (2, 1, 3, 0):
            row = g * RING + d
            chosen = jnp.where(slots[pl.ds(row, 1), :] == slot, 1.0, 0.0).astype(jnp.bfloat16)
            label = (((y + offset_of(g)) % RING) * RING + (x + d) % RING) * 2 + core
            start = start_ref[label]
            tile = jnp.minimum(lax.div(start, jnp.int32(128)), (WIDTH - SPAN) // 128)
            shift = start - tile * 128
            first = tile * 128
            rows = both[:, pl.ds(first, SPAN)]
            picked = jnp.dot(chosen, rows, preferred_element_type=jnp.float32)
            moved = jnp.where(source == target + shift, 1.0, 0.0).astype(jnp.bfloat16)
            picked = jnp.dot(picked.astype(jnp.bfloat16), moved, preferred_element_type=jnp.float32)
            index = jnp.dot(chosen, number, preferred_element_type=jnp.float32)
            last = jnp.where(lane >= SLAB - 384, index, picked[:, 384:512])
            value = jnp.concatenate([picked[:, :384], last], axis=1).astype(jnp.bfloat16)
            if d == 0:
                win[g, z, x] = value
            else:
                packed[row] = value
                wx_copy(g, d).start()

    def take_wz(g):
        for d in (1, 2, 3):
            wx_copy(g, d).wait_recv()
        for way in (0, 1):
            wz_copy(g, way).start()

    def take_wzf(g):
        for way in (0, 1):
            wz_copy(g, way).wait_recv()
            wf_copy(g, way).start()

    def take_exp(g):
        for way in (0, 1):
            wf_copy(g, way).wait_recv()
        token = (lax.broadcasted_iota(jnp.int32, (PAIR, 2 * TOK), 1) + 1).astype(jnp.float32)

        def one(place, total):
            held = win[g, place % RING, place // RING]
            index = held[:, SLAB:SLAB + 1].astype(jnp.float32)
            chosen = jnp.where(index == token, 1.0, 0.0)
            full = lax.dot_general(
                held[:, :SLAB], chosen.astype(jnp.bfloat16), (((0,), (0,)), ((), ())), preferred_element_type=jnp.float32
            ).astype(jnp.bfloat16)
            for side in (0, 1):
                at = pl.multiple_of((side * RING * RING + place) * TOK, 128)
                wide[g, :, pl.ds(at, TOK)] = full[:, side * TOK:(side + 1) * TOK]
            return total + jnp.sum(chosen, axis=0, keepdims=True)

        hits[g] = lax.fori_loop(0, RING * RING, one, jnp.zeros((1, 2 * TOK), jnp.float32), unroll=4)

    def restored(block_q, row_scale):
        return block_q.astype(jnp.int32).astype(jnp.float32) * row_scale

    def take_u(unit):
        g, k = unit // CHUNKS, unit % CHUNKS

        @pl.when(g == 0)
        def _():
            c_copy(k).wait_recv()

        tokens = cols[k].reshape(ROWS, CHUNK)
        part[...] = jnp.dot(wide[g], tokens, preferred_element_type=jnp.float32)

        @pl.when(g == 3)
        def _():
            out_ref[:, pl.ds(pl.multiple_of(k * CHUNK, 128), CHUNK)] = part[...]

        @pl.when(g < 3)
        def _():
            scale[g, k, pl.ds(7, 1), :] = hits[g]

        for way in (0, 1):
            @pl.when(g == 1 + way)
            def _():
                for copy in half_copies(k, way):
                    copy.wait_recv()
                for piece in range(2):
                    rows = pl.ds(way * HALF + piece * SCALE_ROWS, SCALE_ROWS)
                    part[rows, :] += restored(
                        half_q[way, k, pl.ds(piece * SCALE_ROWS, SCALE_ROWS), :],
                        half_s[way, k, pl.ds(2 * way + piece, 1), :],
                    )
                if way == 0:
                    scale[g, k, pl.ds(7, 1), :] = hits[g] + half_s[way, k, pl.ds(7, 1), :]

        @pl.when(g < 3)
        def _():
            for piece in range(SLAB // SCALE_ROWS):
                rows = pl.ds(piece * SCALE_ROWS, SCALE_ROWS)
                block = part[rows, :]
                most = jnp.max(jnp.abs(block), axis=0, keepdims=True)
                factor = jnp.where(most > 0.0, 32767.0 / jnp.where(most > 0.0, most, 1.0), 0.0)
                quant[g, k, rows, :] = jnp.round(block * factor).astype(jnp.int32).astype(jnp.int16)
                scale[g, k, pl.ds(piece, 1), :] = most * (1.0 / 32767.0)

        @pl.when(g == 0)
        def _():
            for way in (0, 1):
                for copy in half_copies(k, way):
                    copy.start()

        @pl.when((g == 1) | (g == 2))
        def _():
            for copy in full_copies(g, k):
                copy.start()

    actions = {
        "S": find_slots, "P": take_p, "XB": take_xb, "XA": take_xa, "Z": send_z, "WZ": take_wz, "WZF": take_wzf, "C": take_c,
        "EXP": take_exp, "U": take_u,
    }
    tables, steps = plan()

    def one_step(step, carry):
        for name in ORDER:
            value = looked_up(tables[name], step)
            pl.when(value >= 0)(functools.partial(actions[name], value))
        return carry

    lax.fori_loop(0, steps, one_step, 0)

    def finish(k, carry):
        for g in (1, 2):
            for copy in full_copies(jnp.int32(g), k):
                copy.wait_recv()
        count = hits[3] + full_s[0, k, pl.ds(7, 1), :] + full_s[1, k, pl.ds(7, 1), :]
        inverse = 1.0 / jnp.sum(count, axis=1, keepdims=True)
        at = pl.ds(pl.multiple_of(k * CHUNK, 128), CHUNK)
        for piece in range(SLAB // SCALE_ROWS):
            rows = pl.ds(piece * SCALE_ROWS, SCALE_ROWS)
            total = out_ref[rows, at]
            for way in (0, 1):
                total += restored(full_q[way, k, rows, :], full_s[way, k, pl.ds(piece, 1), :])
            out_ref[rows, at] = total * inverse
        return carry

    lax.fori_loop(0, CHUNKS, finish, 0)

    for copy in pair_copies():
        copy.wait_send()

    def drain(k, carry):
        for d in (1, 2, 3):
            z_copy(k, d).wait_send()
        for way in (0, 1):
            xa_copy(k, way).wait_send()
            xb_copy(k, way).wait_send()
            for copy in half_copies(k, way):
                copy.wait_send()
        c_copy(k).wait_send()
        for g in (1, 2):
            for copy in full_copies(jnp.int32(g), k):
                copy.wait_send()
        return carry

    lax.fori_loop(0, CHUNKS, drain, 0)

    def drain_windows(g, carry):
        for d in (1, 2, 3):
            wx_copy(g, d).wait_send()
        for way in (0, 1):
            wz_copy(g, way).wait_send()
            wf_copy(g, way).wait_send()
        return carry

    lax.fori_loop(0, GROUPS, drain_windows, 0)


def shards(tokens, routes, slab_start):
    dma = pltpu.SemaphoreType.DMA
    bf16, f32, i16 = jnp.bfloat16, jnp.float32, jnp.int16
    pairs = [(CHUNKS, 2)] * 2
    result = pl.pallas_call(
        gram_kernel,
        out_shape=pltpu.VMEM((SLAB, BLOCK), f32),
        in_specs=[
            pl.BlockSpec(memory_space=pltpu.SMEM),
            pl.BlockSpec(memory_space=pltpu.VMEM),
            pl.BlockSpec(memory_space=pl.ANY),
        ],
        out_specs=pl.BlockSpec(memory_space=pltpu.VMEM),
        scratch_shapes=[
            pltpu.VMEM((2 * TOK, WIDTH), bf16),
            pltpu.VMEM((2, 8, TOK), jnp.int32),
            pltpu.VMEM((GROUPS * RING, 2 * TOK), f32),
            pltpu.VMEM((GROUPS * RING, PAIR, WIDE), bf16),
            pltpu.VMEM((GROUPS, RING, RING, PAIR, WIDE), bf16),
            pltpu.VMEM((GROUPS, SLAB, ROWS), bf16),
            pltpu.VMEM((CHUNKS, 2, RING, RING, TOK, CHUNK), bf16),
            pltpu.VMEM((SLAB, CHUNK), f32),
            pltpu.VMEM((3, CHUNKS, SLAB, CHUNK), i16),
            pltpu.VMEM((3, CHUNKS, 8, CHUNK), f32),
            pltpu.VMEM((2, CHUNKS, HALF, CHUNK), i16),
            pltpu.VMEM((2, CHUNKS, 8, CHUNK), f32),
            pltpu.VMEM((2, CHUNKS, SLAB, CHUNK), i16),
            pltpu.VMEM((2, CHUNKS, 8, CHUNK), f32),
            pltpu.VMEM((GROUPS, 1, 2 * TOK), f32),
            dma((2,)), dma((2,)), dma(()),
            dma((CHUNKS, 3)), dma((CHUNKS, 3)), dma((CHUNKS,)),
            dma((CHUNKS, 2)), dma((CHUNKS, 2)), dma((CHUNKS, 2)), dma((CHUNKS, 2)), dma((CHUNKS,)), dma((CHUNKS,)),
            dma((GROUPS, 3)), dma((GROUPS, 3)), dma((GROUPS, 2)), dma((GROUPS, 2)), dma((GROUPS, 2)), dma((GROUPS, 2)),
            dma((2, CHUNKS)), dma((2, CHUNKS)), dma((2, CHUNKS)), dma((2, CHUNKS)),
            dma((2, CHUNKS)), dma((2, CHUNKS)), dma((2, CHUNKS)), dma((2, CHUNKS)),
        ],
        compiler_params=pltpu.CompilerParams(
            collective_id=0, has_side_effects=True, vmem_limit_bytes=56 * 2**20
        ),
        name="gram",
    )(slab_start, routes.T, tokens)
    return result[None]


def solution(mesh):
    placed = (P(("expert", "dp"), None), P(("expert", "dp"), None), P())
    return jax.shard_map(
        shards, mesh=mesh, in_specs=placed, out_specs=P("expert", None, "dp"), check_vma=False
    )
```

```python
import jax
import jax.numpy as jnp
from jax import lax
from jax.experimental import pallas as pl
from jax.experimental.pallas import tpu as pltpu
from jax.sharding import PartitionSpec as P

MESH = pl.DeviceIdType.MESH
SLAB = 448
CAP = 40
PAIR = 2 * CAP
FULL = 3 * PAIR
TAIL = 48
RING = 4
TOK = 128
WIDTH = 7168
BLOCK = WIDTH // RING
CHUNK = 256
CHUNKS = BLOCK // CHUNK
PLACES = RING * RING
GROUPS = 4
OFFSETS = (2, 1, 3, 0)
SCALE_ROWS = 112
HALF = SLAB // 2
SPAN = 640

CODES = {
    "U": 0, "V": 28, "XO": 42, "XA": 49, "XB": 56, "C": 63, "Z": 70, "P": 77, "WZ": 81, "WZF": 85, "EXP": 89, "S": 93,
}
SCHEDULE = (
    "XO1", "XO5", "Z5", "XO4", "XO0", "S0", "P0", "P2", "WZ0", "P1", "WZ2", "XA1", "WZF0", "XA5", "XA0", "WZ1",
    "WZF2", "XB5", "XB1", "XB0", "P3", "C5", "EXP0", "XO2", "C1", "XA2", "U05", "WZF1", "XO6", "C0", "U01", "Z4",
    "EXP2", "U25", "U00", "Z6", "EXP1", "U15", "U10", "XB2", "V05", "V15", "U20", "XA4", "U21", "C2", "XA6", "WZ3",
    "V11", "U11", "U02", "V10", "V01", "XB4", "Z3", "XB6", "XO3", "V00", "U12", "U22", "C4", "V02", "XA3", "WZF3",
    "C6", "V12", "U06", "U04", "U26", "XB3", "U16", "U24", "U14", "V16", "C3", "EXP3", "U32", "U03", "U23", "U34",
    "V04", "U13", "U30", "V06", "V03", "V13", "U36", "U31", "V14", "U35", "U33",
)


def plan():
    codes = []
    for item in SCHEDULE:
        name = item.rstrip("0123456789")
        digits = item[len(name):]
        value = int(digits[0]) * CHUNKS + int(digits[1]) if len(digits) == 2 else int(digits)
        codes.append(CODES[name] + value)
    padded = codes + [0] * (-len(codes) % 4)
    words = [sum(padded[at + i] * 128 ** i for i in range(4)) for at in range(0, len(padded), 4)]
    return words, len(codes)


def looked_up(words, step):
    word = jnp.int32(words[0])
    for at in range(1, len(words)):
        word = jnp.where(step // 4 == at, jnp.int32(words[at]), word)
    return lax.shift_right_logical(word, 7 * (step % 4)) % 128


def offset_of(group):
    value = jnp.int32(OFFSETS[0])
    for index in range(1, GROUPS):
        value = jnp.where(group == index, jnp.int32(OFFSETS[index]), value)
    return value


def gram_kernel(
    start_ref, routes_ref, tok_ref, out_ref,
    both, listed, slots, packed, win, chosen, wide, cols, near, part, kept, quant, scale, got_q, got_s, hits,
    pair_s, pair_r, own_s, z_s, z_r, zl_s, xo_s, xo_r, xa_s, xa_r, xb_s, xb_r, ca_s, ca_r, c_s, c_r,
    wx_s, wx_r, wz_s, wz_r, wf_s, wf_r, q_s, q_r, f_s, f_r,
):
    expert = lax.axis_index("expert")
    z = lax.axis_index("dp")
    core = expert % 2
    x = (expert // 2) % RING
    y = expert // (2 * RING)

    def device(dy=0, dx=0, dz=0, dc=0):
        ey, ex, ec = (y + dy) % RING, (x + dx) % RING, (core + dc) % 2
        return ((ey * RING + ex) * 2 + ec, (z + dz) % RING)

    def remote(src, dst, send, recv, to):
        return pltpu.make_async_remote_copy(
            src_ref=src, dst_ref=dst, send_sem=send, recv_sem=recv, device_id=to, device_id_type=MESH
        )

    def pair_copies():
        return (
            remote(routes_ref, listed.at[core], pair_s.at[0], pair_r.at[0], device(dc=1)),
            remote(tok_ref, both.at[pl.ds(core * TOK, TOK)], pair_s.at[1], pair_r.at[1], device(dc=1)),
        )

    def own_copy():
        return pltpu.make_async_copy(tok_ref, both.at[pl.ds(core * TOK, TOK)], own_s)

    def z_copy(k, d):
        first = pl.multiple_of(((z + d) % RING) * BLOCK + k * CHUNK, 128)
        return remote(
            tok_ref.at[:, pl.ds(first, CHUNK)], cols.at[k, core, x, z], z_s.at[k, d - 1], z_r.at[k, d - 1], device(dz=d)
        )

    def z_local(k):
        first = pl.multiple_of(z * BLOCK + k * CHUNK, 128)
        return pltpu.make_async_copy(tok_ref.at[:, pl.ds(first, CHUNK)], cols.at[k, core, x, z], zl_s.at[k])

    def xo_copy(k, way):
        here = cols.at[k, core, x, z]
        return remote(here, here, xo_s.at[k, way], xo_r.at[k, way], device(dx=1 if way == 0 else 3))

    def xa_copy(k, way, d):
        here = cols.at[k, core, x, (z + RING - d) % RING]
        return remote(here, here, xa_s.at[k, way, d - 1], xa_r.at[k, way, d - 1], device(dx=1 if way == 0 else 3))

    def xb_copy(k, way):
        origin = (x + (3 if way == 0 else 1)) % RING
        here = cols.at[k, core, origin, pl.ds(2 * way, 2)]
        return remote(here, here, xb_s.at[k, way], xb_r.at[k, way], device(dx=1 if way == 0 else 3))

    def ca_copy(k, d):
        here = cols.at[k, core, (x + d) % RING]
        return remote(here, here, ca_s.at[k, d % RING], ca_r.at[k, d % RING], device(dc=1))

    def c_copy(k):
        here = cols.at[k, core, (x + 2) % RING]
        return remote(here, here, c_s.at[k], c_r.at[k], device(dc=1))

    def wx_copy(g, d):
        return remote(
            packed.at[g * RING + d], win.at[g, z, x], wx_s.at[g, d - 1], wx_r.at[g, d - 1], device(dx=d)
        )

    def wz_copy(g, way):
        here = win.at[g, z]
        return remote(here, here, wz_s.at[g, way], wz_r.at[g, way], device(dz=1 if way == 0 else 3))

    def wf_copy(g, way):
        origin = (z + (3 if way == 0 else 1)) % RING
        here = win.at[g, origin, pl.ds(2 * way, 2)]
        return remote(here, here, wf_s.at[g, way], wf_r.at[g, way], device(dz=1 if way == 0 else 3))

    def sum_copies(way, slot, k):
        to = device(dy=1 if way == 0 else 3)
        values = remote(quant.at[way, slot, k], got_q.at[way, slot, k], q_s.at[way, slot, k], q_r.at[way, slot, k], to)
        if slot == 1:
            return (values,)
        at = slot // 2
        return (values, remote(scale.at[way, at, k], got_s.at[way, at, k], f_s.at[way, at, k], f_r.at[way, at, k], to))

    barrier = pltpu.get_barrier_semaphore()
    peers = [device(dc=1), device(dy=1), device(dy=3)]
    peers += [device(dx=d) for d in (1, 2, 3)] + [device(dz=d) for d in (1, 2, 3)]
    for peer in peers:
        pl.semaphore_signal(barrier, inc=1, device_id=peer, device_id_type=MESH)
    pl.semaphore_wait(barrier, len(peers))

    def send_z(k):
        for d in (1, 3, 2):
            z_copy(k, d).start()

    for copy in pair_copies():
        copy.start()
    own_copy().start()
    for k in range(3):
        send_z(jnp.int32(k))
    for k in range(CHUNKS):
        z_local(k).start()
    listed[core] = routes_ref[...]

    def take_xo(k):
        z_local(k).wait()
        for way in (0, 1):
            xo_copy(k, way).start()

    def take_xa(k):
        for d in (1, 3, 2):
            z_copy(k, d).wait_recv()
            for way in (0, 1):
                xa_copy(k, way, d).start()

    def take_xb(k):
        for way in (0, 1):
            xo_copy(k, way).wait_recv()
            for d in (1, 2, 3):
                xa_copy(k, way, d).wait_recv()
            xb_copy(k, way).start()
        for d in (0, 1, 3):
            ca_copy(k, d).start()

    def take_c(k):
        for way in (0, 1):
            xb_copy(k, way).wait_recv()
        c_copy(k).start()

    def find_slots(_):
        for copy in pair_copies():
            copy.wait_recv()
        own_copy().wait()
        named = jnp.concatenate([listed[0], listed[1]], axis=1)
        row = lax.broadcasted_iota(jnp.int32, (GROUPS * RING, 2 * TOK), 0)
        group, step = row // RING, row % RING
        away = jnp.where(group == 0, OFFSETS[0], jnp.where(group == 1, OFFSETS[1], jnp.where(group == 2, OFFSETS[2], OFFSETS[3])))
        label = (((y + away) % RING) * RING + (x + step) % RING) * 2 + core
        hit = jnp.zeros((GROUPS * RING, 2 * TOK), jnp.float32)
        for choice in range(named.shape[0]):
            hit += jnp.where(named[choice:choice + 1, :] == label, 1.0, 0.0)
        before = lax.broadcasted_iota(jnp.int32, (2 * TOK, 2 * TOK), 0) < lax.broadcasted_iota(
            jnp.int32, (2 * TOK, 2 * TOK), 1
        )
        rank = jnp.dot(
            hit.astype(jnp.bfloat16), jnp.where(before, 1.0, 0.0).astype(jnp.bfloat16), preferred_element_type=jnp.float32
        )
        slots[...] = jnp.where(hit > 0.0, rank, -1.0)

    def take_p(g):
        slot = lax.broadcasted_iota(jnp.int32, (PAIR, 2 * TOK), 0).astype(jnp.float32)
        source = lax.broadcasted_iota(jnp.int32, (SPAN, 512), 0)
        target = lax.broadcasted_iota(jnp.int32, (SPAN, 512), 1)
        for d in (2, 1, 3, 0):
            row = g * RING + d
            taken = jnp.where(slots[pl.ds(row, 1), :] == slot, 1.0, 0.0).astype(jnp.bfloat16)
            label = (((y + offset_of(g)) % RING) * RING + (x + d) % RING) * 2 + core
            start = start_ref[label]
            tile = jnp.minimum(lax.div(start, jnp.int32(128)), (WIDTH - SPAN) // 128)
            shift = start - tile * 128
            first = tile * 128
            rows = both[:, pl.ds(first, SPAN)]
            picked = jnp.dot(taken, rows, preferred_element_type=jnp.float32)
            moved = jnp.where(source == target + shift, 1.0, 0.0).astype(jnp.bfloat16)
            picked = jnp.dot(picked.astype(jnp.bfloat16), moved, preferred_element_type=jnp.float32)
            rest = picked[:, 384:SLAB]
            seat = slots[pl.ds(row, 1), :]
            seats = [seat[:, 64 * part:64 * part + 64] for part in range(4)] + [jnp.zeros((12, 64), jnp.float32)]
            tail = jnp.concatenate([rest[:TAIL], jnp.concatenate([rest[TAIL:]] + seats, axis=0)], axis=1)
            blocks = [picked[:, 128 * tile:128 * tile + 128] for tile in range(3)] + [tail]
            value = jnp.concatenate(blocks, axis=0).astype(jnp.bfloat16)
            if d == 0:
                win[g, z, x] = value
            else:
                packed[row] = value
                wx_copy(g, d).start()

    def take_wz(g):
        for d in (1, 2, 3):
            wx_copy(g, d).wait_recv()
        for way in (0, 1):
            wz_copy(g, way).start()

    def take_wzf(g):
        for way in (0, 1):
            wz_copy(g, way).wait_recv()
            wf_copy(g, way).start()

    def take_exp(g):
        for way in (0, 1):
            wf_copy(g, way).wait_recv()
        slot = lax.broadcasted_iota(jnp.int32, (PAIR, 2 * TOK), 0).astype(jnp.float32)
        total = jnp.zeros((1, 2 * TOK), jnp.float32)
        rests = []
        for place in range(PLACES):
            tail = win[g, place // RING, place % RING, FULL:, :].astype(jnp.float32)
            first, second = tail[:, :64], tail[:, 64:]
            rests.append(jnp.concatenate([first, second[:PAIR - TAIL]], axis=0))
            at = PAIR - TAIL
            seat = jnp.concatenate([second[at + part:at + part + 1] for part in range(4)], axis=1)
            chosen[g, place] = jnp.where(seat == slot, 1.0, 0.0).astype(jnp.bfloat16)
            total += jnp.where(seat >= 0.0, 1.0, 0.0)
        hits[g] = total
        for tile in range(3):
            block = win[g, :, :, tile * PAIR:(tile + 1) * PAIR, :].reshape(PLACES * PAIR, 128)
            wide[g, tile * 128:(tile + 1) * 128, :] = block.T
        wide[g, 384:, :] = jnp.concatenate(rests, axis=0).astype(jnp.bfloat16).T

    def scale_row(slot, piece):
        return (slot + 1) // 2, pl.ds(piece + (2 if slot == 1 else 0), 1)

    def restored(way, slot, k, piece):
        block = got_q[way, slot, k, pl.ds(piece * SCALE_ROWS, SCALE_ROWS), :]
        at, row = scale_row(slot, piece)
        return block.astype(jnp.int32).astype(jnp.float32) * got_s[way, at, k, row, :]

    def send_sum(way, slot, k, pieces, count):
        for piece, block in enumerate(pieces):
            most = jnp.max(jnp.abs(block), axis=0, keepdims=True)
            factor = jnp.where(most > 0.0, 32767.0 / jnp.where(most > 0.0, most, 1.0), 0.0)
            rows = pl.ds(piece * SCALE_ROWS, SCALE_ROWS)
            quant[way, slot, k, rows, :] = jnp.round(block * factor).astype(jnp.int32).astype(jnp.int16)
            at, row = scale_row(slot, piece)
            scale[way, at, k, row, :] = most * (1.0 / 32767.0)
        if count is not None:
            scale[way, slot // 2, k, pl.ds(7, 1), :] = count
        for copy in sum_copies(way, slot, k):
            copy.start()

    def take_u(unit):
        g, k = unit // CHUNKS, unit % CHUNKS

        @pl.when(g == 0)
        def _():
            for d in (0, 1, 3):
                ca_copy(k, d).wait_recv()
            c_copy(k).wait_recv()

        for place in range(PLACES):
            from_x, from_z = place % RING, place // RING
            tokens = jnp.concatenate([cols[k, 0, from_x, from_z], cols[k, 1, from_x, from_z]], axis=0)
            near[pl.ds(place * PAIR, PAIR), :] = jnp.dot(
                chosen[g, place], tokens, preferred_element_type=jnp.float32
            ).astype(jnp.bfloat16)
        part[...] = jnp.dot(wide[g], near[...], preferred_element_type=jnp.float32)

        def pieces(half):
            first = half * HALF
            return [part[first + SCALE_ROWS * piece:first + SCALE_ROWS * (piece + 1), :] for piece in range(2)]

        @pl.when(g == 0)
        def _():
            for way in (0, 1):
                send_sum(way, 0, k, pieces(way), hits[g])

        for way in (0, 1):
            @pl.when(g == 1 + way)
            def _():
                send_sum(way, 1, k, pieces(1 - way), None)
                kept[way, k] = part[way * HALF:(way + 1) * HALF, :]

        @pl.when(g == 3)
        def _():
            out_ref[:, pl.ds(pl.multiple_of(k * CHUNK, 128), CHUNK)] = part[...]

    def take_v(unit):
        k = unit % CHUNKS
        for way in (0, 1):
            @pl.when(unit // CHUNKS == way)
            def _():
                for copy in sum_copies(way, 0, k):
                    copy.wait_recv()
                pieces = [
                    kept[way, k, pl.ds(piece * SCALE_ROWS, SCALE_ROWS), :] + restored(way, 0, k, piece)
                    for piece in range(2)
                ]
                below = got_s[way, 0, k, pl.ds(7, 1), :]
                send_sum(way, 2, k, pieces, hits[1] + below if way == 0 else hits[2])

    actions = {
        "S": find_slots, "P": take_p, "XO": take_xo, "XA": take_xa, "XB": take_xb, "Z": send_z, "WZ": take_wz,
        "WZF": take_wzf, "C": take_c, "EXP": take_exp, "U": take_u, "V": take_v,
    }
    words, length = plan()

    def one_step(step, carry):
        code = looked_up(words, step)

        def among(names):
            if len(names) == 1:
                actions[names[0]](code - CODES[names[0]])
                return
            middle = len(names) // 2
            low = code < CODES[names[middle]]
            pl.when(low)(lambda: among(names[:middle]))
            pl.when(jnp.logical_not(low))(lambda: among(names[middle:]))

        among(list(CODES))
        return carry

    lax.fori_loop(0, length, one_step, 0)

    def finish(k, carry):
        for way in (0, 1):
            for slot in (1, 2):
                for copy in sum_copies(way, slot, k):
                    copy.wait_recv()
        count = hits[3] + got_s[0, 1, k, pl.ds(7, 1), :] + got_s[1, 1, k, pl.ds(7, 1), :]
        inverse = 1.0 / jnp.sum(count, axis=1, keepdims=True)
        at = pl.ds(pl.multiple_of(k * CHUNK, 128), CHUNK)
        for half in (0, 1):
            for piece in (0, 1):
                rows = pl.ds(half * HALF + piece * SCALE_ROWS, SCALE_ROWS)
                total = out_ref[rows, at] + restored(half, 2, k, piece) + restored(1 - half, 1, k, piece)
                out_ref[rows, at] = total * inverse
        return carry

    lax.fori_loop(0, CHUNKS, finish, 0)

    for copy in pair_copies():
        copy.wait_send()

    def drain(k, carry):
        for d in (1, 2, 3):
            z_copy(k, d).wait_send()
            for way in (0, 1):
                xa_copy(k, way, d).wait_send()
        for d in (0, 1, 3):
            ca_copy(k, d).wait_send()
        c_copy(k).wait_send()
        for way in (0, 1):
            xo_copy(k, way).wait_send()
            xb_copy(k, way).wait_send()
            for slot in range(3):
                for copy in sum_copies(way, slot, k):
                    copy.wait_send()
        return carry

    lax.fori_loop(0, CHUNKS, drain, 0)

    def drain_windows(g, carry):
        for d in (1, 2, 3):
            wx_copy(g, d).wait_send()
        for way in (0, 1):
            wz_copy(g, way).wait_send()
            wf_copy(g, way).wait_send()
        return carry

    lax.fori_loop(0, GROUPS, drain_windows, 0)


def shards(tokens, routes, slab_start):
    dma = pltpu.SemaphoreType.DMA
    bf16, f32, i16 = jnp.bfloat16, jnp.float32, jnp.int16
    result = pl.pallas_call(
        gram_kernel,
        out_shape=pltpu.VMEM((SLAB, BLOCK), f32),
        in_specs=[
            pl.BlockSpec(memory_space=pltpu.SMEM),
            pl.BlockSpec(memory_space=pltpu.VMEM),
            pl.BlockSpec(memory_space=pl.ANY),
        ],
        out_specs=pl.BlockSpec(memory_space=pltpu.VMEM),
        scratch_shapes=[
            pltpu.VMEM((2 * TOK, WIDTH), bf16),
            pltpu.VMEM((2, 8, TOK), jnp.int32),
            pltpu.VMEM((GROUPS * RING, 2 * TOK), f32),
            pltpu.VMEM((GROUPS * RING, FULL + TAIL, 128), bf16),
            pltpu.VMEM((GROUPS, RING, RING, FULL + TAIL, 128), bf16),
            pltpu.VMEM((GROUPS, PLACES, PAIR, 2 * TOK), bf16),
            pltpu.VMEM((GROUPS, SLAB, PLACES * PAIR), bf16),
            pltpu.VMEM((CHUNKS, 2, RING, RING, TOK, CHUNK), bf16),
            pltpu.VMEM((PLACES * PAIR, CHUNK), bf16),
            pltpu.VMEM((SLAB, CHUNK), f32),
            pltpu.VMEM((2, CHUNKS, HALF, CHUNK), f32),
            pltpu.VMEM((2, 3, CHUNKS, HALF, CHUNK), i16),
            pltpu.VMEM((2, 2, CHUNKS, 8, CHUNK), f32),
            pltpu.VMEM((2, 3, CHUNKS, HALF, CHUNK), i16),
            pltpu.VMEM((2, 2, CHUNKS, 8, CHUNK), f32),
            pltpu.VMEM((GROUPS, 1, 2 * TOK), f32),
            dma((2,)), dma((2,)), dma(()),
            dma((CHUNKS, 3)), dma((CHUNKS, 3)), dma((CHUNKS,)),
            dma((CHUNKS, 2)), dma((CHUNKS, 2)), dma((CHUNKS, 2, 3)), dma((CHUNKS, 2, 3)), dma((CHUNKS, 2)), dma((CHUNKS, 2)),
            dma((CHUNKS, 4)), dma((CHUNKS, 4)), dma((CHUNKS,)), dma((CHUNKS,)),
            dma((GROUPS, 3)), dma((GROUPS, 3)), dma((GROUPS, 2)), dma((GROUPS, 2)), dma((GROUPS, 2)), dma((GROUPS, 2)),
            dma((2, 3, CHUNKS)), dma((2, 3, CHUNKS)), dma((2, 2, CHUNKS)), dma((2, 2, CHUNKS)),
        ],
        compiler_params=pltpu.CompilerParams(
            collective_id=0, has_side_effects=True, vmem_limit_bytes=56 * 2**20
        ),
        name="gram",
    )(slab_start, routes.T, tokens)
    return result[None]


def solution(mesh):
    placed = (P(("expert", "dp"), None), P(("expert", "dp"), None), P())
    return jax.shard_map(
        shards, mesh=mesh, in_specs=placed, out_specs=P("expert", None, "dp"), check_vma=False
    )
```

```python
import jax
import jax.numpy as jnp
from jax import lax
from jax.experimental import pallas as pl
from jax.experimental.pallas import tpu as pltpu
from jax.sharding import PartitionSpec as P

MESH = pl.DeviceIdType.MESH
SLAB = 448
CAP = 40
PAIR = 2 * CAP
FULL = 3 * PAIR
TAIL = 48
RING = 4
TOK = 128
WIDTH = 7168
BLOCK = WIDTH // RING
CHUNK = 256
CHUNKS = BLOCK // CHUNK
PLACES = RING * RING
GROUPS = 4
OFFSETS = (2, 1, 3, 0)
SCALE_ROWS = 112
HALF = SLAB // 2
SPAN = 640

CODES = {
    "U": 0, "V": 28, "XO": 42, "XA": 49, "XB": 56, "C": 63, "Z": 70, "P": 77, "WZ": 81, "WZF": 85, "EXP": 89, "S": 93,
}
SCHEDULE = (
    "XO1", "XO2", "XO0", "Z5", "XA0", "S0", "P0", "P2", "XB0", "WZ0", "XA1", "WZ2", "WZF0", "C0", "P1", "XA2",
    "XB1", "WZ1", "WZF2", "EXP0", "U00", "XB2", "XO5", "P3", "C1", "WZF1", "Z4", "XO4", "XO3", "XA5", "C2", "U01",
    "EXP2", "U02", "U21", "EXP1", "U11", "XA4", "V11", "V01", "Z3", "U10", "V00", "U20", "XB5", "Z6", "U22", "XB4",
    "U12", "XO6", "V10", "C5", "V12", "WZ3", "V02", "XA3", "XA6", "C4", "U05", "U25", "U04", "U15", "WZF3", "U14",
    "XB3", "U24", "V05", "V04", "XB6", "V15", "EXP3", "V14", "C3", "U34", "U35", "C6", "U03", "U13", "U06", "U23",
    "U33", "V03", "V13", "U32", "U16", "U26", "V16", "V06", "U30", "U36", "U31",
)


def plan():
    codes = []
    for item in SCHEDULE:
        name = item.rstrip("0123456789")
        digits = item[len(name):]
        value = int(digits[0]) * CHUNKS + int(digits[1]) if len(digits) == 2 else int(digits)
        codes.append(CODES[name] + value)
    padded = codes + [0] * (-len(codes) % 4)
    words = [sum(padded[at + i] * 128 ** i for i in range(4)) for at in range(0, len(padded), 4)]
    return words, len(codes)


def looked_up(words, step):
    word = jnp.int32(words[0])
    for at in range(1, len(words)):
        word = jnp.where(step // 4 == at, jnp.int32(words[at]), word)
    return lax.shift_right_logical(word, 7 * (step % 4)) % 128


def offset_of(group):
    value = jnp.int32(OFFSETS[0])
    for index in range(1, GROUPS):
        value = jnp.where(group == index, jnp.int32(OFFSETS[index]), value)
    return value


def gram_kernel(
    start_ref, routes_ref, tok_ref, out_ref,
    both, listed, slots, packed, win, chosen, wide, cols, near, part, kept, quant, scale, got_q, got_s, hits,
    pair_s, pair_r, own_s, z_s, z_r, zl_s, xo_s, xo_r, xa_s, xa_r, xb_s, xb_r, ca_s, ca_r, c_s, c_r,
    wx_s, wx_r, wz_s, wz_r, wf_s, wf_r, q_s, q_r, f_s, f_r,
):
    expert = lax.axis_index("expert")
    z = lax.axis_index("dp")
    core = expert % 2
    x = (expert // 2) % RING
    y = expert // (2 * RING)

    def device(dy=0, dx=0, dz=0, dc=0):
        ey, ex, ec = (y + dy) % RING, (x + dx) % RING, (core + dc) % 2
        return ((ey * RING + ex) * 2 + ec, (z + dz) % RING)

    def remote(src, dst, send, recv, to):
        return pltpu.make_async_remote_copy(
            src_ref=src, dst_ref=dst, send_sem=send, recv_sem=recv, device_id=to, device_id_type=MESH
        )

    def pair_copies():
        return (
            remote(routes_ref, listed.at[core], pair_s.at[0], pair_r.at[0], device(dc=1)),
            remote(tok_ref, both.at[pl.ds(core * TOK, TOK)], pair_s.at[1], pair_r.at[1], device(dc=1)),
        )

    def own_copy():
        return pltpu.make_async_copy(tok_ref, both.at[pl.ds(core * TOK, TOK)], own_s)

    def z_copy(k, d):
        first = pl.multiple_of(((z + d) % RING) * BLOCK + k * CHUNK, 128)
        return remote(
            tok_ref.at[:, pl.ds(first, CHUNK)], cols.at[k, core, x, z], z_s.at[k, d - 1], z_r.at[k, d - 1], device(dz=d)
        )

    def z_local(k):
        first = pl.multiple_of(z * BLOCK + k * CHUNK, 128)
        return pltpu.make_async_copy(tok_ref.at[:, pl.ds(first, CHUNK)], cols.at[k, core, x, z], zl_s.at[k])

    def xo_copy(k, way):
        here = cols.at[k, core, x, z]
        return remote(here, here, xo_s.at[k, way], xo_r.at[k, way], device(dx=1 if way == 0 else 3))

    def xa_copy(k, way, d):
        here = cols.at[k, core, x, (z + RING - d) % RING]
        return remote(here, here, xa_s.at[k, way, d - 1], xa_r.at[k, way, d - 1], device(dx=1 if way == 0 else 3))

    def xb_copy(k, way):
        origin = (x + (3 if way == 0 else 1)) % RING
        here = cols.at[k, core, origin, pl.ds(2 * way, 2)]
        return remote(here, here, xb_s.at[k, way], xb_r.at[k, way], device(dx=1 if way == 0 else 3))

    def ca_copy(k, d):
        here = cols.at[k, core, (x + d) % RING]
        return remote(here, here, ca_s.at[k, d % RING], ca_r.at[k, d % RING], device(dc=1))

    def c_copy(k):
        here = cols.at[k, core, (x + 2) % RING]
        return remote(here, here, c_s.at[k], c_r.at[k], device(dc=1))

    def wx_copy(g, d):
        return remote(
            packed.at[g * RING + d], win.at[g, z, x], wx_s.at[g, d - 1], wx_r.at[g, d - 1], device(dx=d)
        )

    def wz_copy(g, way, d):
        here = win.at[g, z, (x + RING - d) % RING]
        return remote(here, here, wz_s.at[g, way, d], wz_r.at[g, way, d], device(dz=1 if way == 0 else 3))

    def wf_copy(g, way, d):
        here = win.at[g, (z + (3 if way == 0 else 1)) % RING, (x + RING - d) % RING]
        return remote(here, here, wf_s.at[g, way, d % 2], wf_r.at[g, way, d % 2], device(dz=1 if way == 0 else 3))

    def sum_copies(way, slot, k):
        to = device(dy=1 if way == 0 else 3)
        values = remote(quant.at[way, slot, k], got_q.at[way, slot, k], q_s.at[way, slot, k], q_r.at[way, slot, k], to)
        if slot == 1:
            return (values,)
        at = slot // 2
        return (values, remote(scale.at[way, at, k], got_s.at[way, at, k], f_s.at[way, at, k], f_r.at[way, at, k], to))

    for k in range(CHUNKS):
        z_local(k).start()
    own_copy().start()

    barrier = pltpu.get_barrier_semaphore()
    peers = [device(dc=1), device(dy=1), device(dy=3)]
    peers += [device(dx=d) for d in (1, 2, 3)] + [device(dz=d) for d in (1, 2, 3)]
    for peer in peers:
        pl.semaphore_signal(barrier, inc=1, device_id=peer, device_id_type=MESH)
    pl.semaphore_wait(barrier, len(peers))

    def send_z(k):
        for d in (1, 3, 2):
            z_copy(k, d).start()

    for copy in pair_copies():
        copy.start()
    for k in range(3):
        send_z(jnp.int32(k))
    listed[core] = routes_ref[...]

    def take_xo(k):
        z_local(k).wait()
        for way in (0, 1):
            xo_copy(k, way).start()

    def take_xa(k):
        for d in (1, 3, 2):
            z_copy(k, d).wait_recv()
            for way in (0, 1):
                xa_copy(k, way, d).start()

    def take_xb(k):
        for way in (0, 1):
            xo_copy(k, way).wait_recv()
            for d in (1, 2, 3):
                xa_copy(k, way, d).wait_recv()
            xb_copy(k, way).start()
        for d in (0, 1, 3):
            ca_copy(k, d).start()

    def take_c(k):
        for way in (0, 1):
            xb_copy(k, way).wait_recv()
        c_copy(k).start()

    def find_slots(_):
        for copy in pair_copies():
            copy.wait_recv()
        own_copy().wait()
        named = jnp.concatenate([listed[0], listed[1]], axis=1)
        row = lax.broadcasted_iota(jnp.int32, (GROUPS * RING, 2 * TOK), 0)
        group, step = row // RING, row % RING
        away = jnp.where(group == 0, OFFSETS[0], jnp.where(group == 1, OFFSETS[1], jnp.where(group == 2, OFFSETS[2], OFFSETS[3])))
        label = (((y + away) % RING) * RING + (x + step) % RING) * 2 + core
        hit = jnp.zeros((GROUPS * RING, 2 * TOK), jnp.float32)
        for choice in range(named.shape[0]):
            hit += jnp.where(named[choice:choice + 1, :] == label, 1.0, 0.0)
        before = lax.broadcasted_iota(jnp.int32, (2 * TOK, 2 * TOK), 0) < lax.broadcasted_iota(
            jnp.int32, (2 * TOK, 2 * TOK), 1
        )
        rank = jnp.dot(
            hit.astype(jnp.bfloat16), jnp.where(before, 1.0, 0.0).astype(jnp.bfloat16), preferred_element_type=jnp.float32
        )
        slots[...] = jnp.where(hit > 0.0, rank, -1.0)

    def take_p(g):
        slot = lax.broadcasted_iota(jnp.int32, (PAIR, 2 * TOK), 0).astype(jnp.float32)
        source = lax.broadcasted_iota(jnp.int32, (SPAN, 512), 0)
        target = lax.broadcasted_iota(jnp.int32, (SPAN, 512), 1)
        for d in (2, 1, 3, 0):
            row = g * RING + d
            taken = jnp.where(slots[pl.ds(row, 1), :] == slot, 1.0, 0.0).astype(jnp.bfloat16)
            label = (((y + offset_of(g)) % RING) * RING + (x + d) % RING) * 2 + core
            start = start_ref[label]
            tile = jnp.minimum(lax.div(start, jnp.int32(128)), (WIDTH - SPAN) // 128)
            shift = start - tile * 128
            first = tile * 128
            rows = both[:, pl.ds(first, SPAN)]
            picked = jnp.dot(taken, rows, preferred_element_type=jnp.float32)
            moved = jnp.where(source == target + shift, 1.0, 0.0).astype(jnp.bfloat16)
            picked = jnp.dot(picked.astype(jnp.bfloat16), moved, preferred_element_type=jnp.float32)
            rest = picked[:, 384:SLAB]
            seat = slots[pl.ds(row, 1), :]
            seats = [seat[:, 64 * part:64 * part + 64] for part in range(4)] + [jnp.zeros((12, 64), jnp.float32)]
            tail = jnp.concatenate([rest[:TAIL], jnp.concatenate([rest[TAIL:]] + seats, axis=0)], axis=1)
            blocks = [picked[:, 128 * tile:128 * tile + 128] for tile in range(3)] + [tail]
            value = jnp.concatenate(blocks, axis=0).astype(jnp.bfloat16)
            if d == 0:
                win[g, z, x] = value
                for way in (0, 1):
                    wz_copy(g, way, 0).start()
            else:
                packed[row] = value
                wx_copy(g, d).start()

    def take_wz(g):
        for d in (1, 3, 2):
            wx_copy(g, d).wait_recv()
            for way in (0, 1):
                wz_copy(g, way, d).start()

    def take_wzf(g):
        for way in (0, 1):
            for d in (2 * way, 2 * way + 1):
                wz_copy(g, way, d).wait_recv()
                wf_copy(g, way, d).start()

    def take_exp(g):
        for way in (0, 1):
            for d in (2 * way, 2 * way + 1):
                wz_copy(g, 1 - way, d).wait_recv()
                wf_copy(g, way, d).wait_recv()
        slot = lax.broadcasted_iota(jnp.int32, (PAIR, 2 * TOK), 0).astype(jnp.float32)
        total = jnp.zeros((1, 2 * TOK), jnp.float32)
        rests = []
        for place in range(PLACES):
            tail = win[g, place // RING, place % RING, FULL:, :].astype(jnp.float32)
            first, second = tail[:, :64], tail[:, 64:]
            rests.append(jnp.concatenate([first, second[:PAIR - TAIL]], axis=0))
            at = PAIR - TAIL
            seat = jnp.concatenate([second[at + part:at + part + 1] for part in range(4)], axis=1)
            chosen[g, place] = jnp.where(seat == slot, 1.0, 0.0).astype(jnp.bfloat16)
            total += jnp.where(seat >= 0.0, 1.0, 0.0)
        hits[g] = total[:, :TOK] + total[:, TOK:]
        for tile in range(3):
            block = win[g, :, :, tile * PAIR:(tile + 1) * PAIR, :].reshape(PLACES * PAIR, 128)
            wide[g, tile * 128:(tile + 1) * 128, :] = block.T
        wide[g, 384:, :] = jnp.concatenate(rests, axis=0).astype(jnp.bfloat16).T

    def scale_row(slot, piece):
        return (slot + 1) // 2, pl.ds(piece + (2 if slot == 1 else 0), 1)

    def restored(way, slot, k, piece):
        block = got_q[way, slot, k, pl.ds(piece * SCALE_ROWS, SCALE_ROWS), :]
        at, row = scale_row(slot, piece)
        factor = got_s[way, at, k, row, :]
        return block.astype(jnp.int32).astype(jnp.float32) * jnp.concatenate([factor, factor], axis=1)

    def send_sum(way, slot, k, pieces, count):
        for piece, block in enumerate(pieces):
            most = jnp.max(jnp.abs(block), axis=0, keepdims=True)
            most = jnp.maximum(most[:, :128], most[:, 128:])
            factor = jnp.where(most > 0.0, 32767.0 / jnp.where(most > 0.0, most, 1.0), 0.0)
            factor = jnp.concatenate([factor, factor], axis=1)
            rows = pl.ds(piece * SCALE_ROWS, SCALE_ROWS)
            quant[way, slot, k, rows, :] = jnp.round(block * factor).astype(jnp.int32).astype(jnp.int16)
            at, row = scale_row(slot, piece)
            scale[way, at, k, row, :] = most * (1.0 / 32767.0)
        if count is not None:
            scale[way, slot // 2, k, pl.ds(7, 1), :] = count
        for copy in sum_copies(way, slot, k):
            copy.start()

    def take_u(unit):
        g, k = unit // CHUNKS, unit % CHUNKS

        @pl.when(g == 0)
        def _():
            for d in (0, 1, 3):
                ca_copy(k, d).wait_recv()
            c_copy(k).wait_recv()

        for place in range(PLACES):
            from_x, from_z = place % RING, place // RING
            tokens = jnp.concatenate([cols[k, 0, from_x, from_z], cols[k, 1, from_x, from_z]], axis=0)
            near[pl.ds(place * PAIR, PAIR), :] = jnp.dot(
                chosen[g, place], tokens, preferred_element_type=jnp.float32
            ).astype(jnp.bfloat16)
        part[...] = jnp.dot(wide[g], near[...], preferred_element_type=jnp.float32)

        def pieces(half):
            first = half * HALF
            return [part[first + SCALE_ROWS * piece:first + SCALE_ROWS * (piece + 1), :] for piece in range(2)]

        @pl.when(g == 0)
        def _():
            for way in (0, 1):
                send_sum(way, 0, k, pieces(way), hits[g])

        for way in (0, 1):
            @pl.when(g == 1 + way)
            def _():
                send_sum(way, 1, k, pieces(1 - way), None)
                kept[way, k] = part[way * HALF:(way + 1) * HALF, :]

        @pl.when(g == 3)
        def _():
            out_ref[:, pl.ds(pl.multiple_of(k * CHUNK, 128), CHUNK)] = part[...]

    def take_v(unit):
        k = unit % CHUNKS
        for way in (0, 1):
            @pl.when(unit // CHUNKS == way)
            def _():
                for copy in sum_copies(way, 0, k):
                    copy.wait_recv()
                pieces = [
                    kept[way, k, pl.ds(piece * SCALE_ROWS, SCALE_ROWS), :] + restored(way, 0, k, piece)
                    for piece in range(2)
                ]
                below = got_s[way, 0, k, pl.ds(7, 1), :]
                send_sum(way, 2, k, pieces, hits[1] + below if way == 0 else hits[2])

    actions = {
        "S": find_slots, "P": take_p, "XO": take_xo, "XA": take_xa, "XB": take_xb, "Z": send_z, "WZ": take_wz,
        "WZF": take_wzf, "C": take_c, "EXP": take_exp, "U": take_u, "V": take_v,
    }
    words, length = plan()

    def one_step(step, carry):
        code = looked_up(words, step)

        def among(names):
            if len(names) == 1:
                actions[names[0]](code - CODES[names[0]])
                return
            middle = len(names) // 2
            low = code < CODES[names[middle]]
            pl.when(low)(lambda: among(names[:middle]))
            pl.when(jnp.logical_not(low))(lambda: among(names[middle:]))

        among(list(CODES))
        return carry

    lax.fori_loop(0, length, one_step, 0)

    def finish(k, carry):
        for way in (0, 1):
            for slot in (1, 2):
                for copy in sum_copies(way, slot, k):
                    copy.wait_recv()
        count = hits[3] + got_s[0, 1, k, pl.ds(7, 1), :] + got_s[1, 1, k, pl.ds(7, 1), :]
        inverse = 1.0 / jnp.sum(count, axis=1, keepdims=True)
        at = pl.ds(pl.multiple_of(k * CHUNK, 128), CHUNK)
        for half in (0, 1):
            for piece in (0, 1):
                rows = pl.ds(half * HALF + piece * SCALE_ROWS, SCALE_ROWS)
                total = out_ref[rows, at] + restored(half, 2, k, piece) + restored(1 - half, 1, k, piece)
                out_ref[rows, at] = total * inverse
        return carry

    lax.fori_loop(0, CHUNKS, finish, 0)

    for copy in pair_copies():
        copy.wait_send()

    def drain(k, carry):
        for d in (1, 2, 3):
            z_copy(k, d).wait_send()
            for way in (0, 1):
                xa_copy(k, way, d).wait_send()
        for d in (0, 1, 3):
            ca_copy(k, d).wait_send()
        c_copy(k).wait_send()
        for way in (0, 1):
            xo_copy(k, way).wait_send()
            xb_copy(k, way).wait_send()
            for slot in range(3):
                for copy in sum_copies(way, slot, k):
                    copy.wait_send()
        return carry

    lax.fori_loop(0, CHUNKS, drain, 0)

    def drain_windows(g, carry):
        for d in (1, 2, 3):
            wx_copy(g, d).wait_send()
        for way in (0, 1):
            for d in range(RING):
                wz_copy(g, way, d).wait_send()
            for d in (2 * way, 2 * way + 1):
                wf_copy(g, way, d).wait_send()
        return carry

    lax.fori_loop(0, GROUPS, drain_windows, 0)


def shards(tokens, routes, slab_start):
    dma = pltpu.SemaphoreType.DMA
    bf16, f32, i16 = jnp.bfloat16, jnp.float32, jnp.int16
    result = pl.pallas_call(
        gram_kernel,
        out_shape=pltpu.VMEM((SLAB, BLOCK), f32),
        in_specs=[
            pl.BlockSpec(memory_space=pltpu.SMEM),
            pl.BlockSpec(memory_space=pltpu.VMEM),
            pl.BlockSpec(memory_space=pl.ANY),
        ],
        out_specs=pl.BlockSpec(memory_space=pltpu.VMEM),
        scratch_shapes=[
            pltpu.VMEM((2 * TOK, WIDTH), bf16),
            pltpu.VMEM((2, 8, TOK), jnp.int32),
            pltpu.VMEM((GROUPS * RING, 2 * TOK), f32),
            pltpu.VMEM((GROUPS * RING, FULL + TAIL, 128), bf16),
            pltpu.VMEM((GROUPS, RING, RING, FULL + TAIL, 128), bf16),
            pltpu.VMEM((GROUPS, PLACES, PAIR, 2 * TOK), bf16),
            pltpu.VMEM((GROUPS, SLAB, PLACES * PAIR), bf16),
            pltpu.VMEM((CHUNKS, 2, RING, RING, TOK, CHUNK), bf16),
            pltpu.VMEM((PLACES * PAIR, CHUNK), bf16),
            pltpu.VMEM((SLAB, CHUNK), f32),
            pltpu.VMEM((2, CHUNKS, HALF, CHUNK), f32),
            pltpu.VMEM((2, 3, CHUNKS, HALF, CHUNK), i16),
            pltpu.VMEM((2, 2, CHUNKS, 8, 128), f32),
            pltpu.VMEM((2, 3, CHUNKS, HALF, CHUNK), i16),
            pltpu.VMEM((2, 2, CHUNKS, 8, 128), f32),
            pltpu.VMEM((GROUPS, 1, TOK), f32),
            dma((2,)), dma((2,)), dma(()),
            dma((CHUNKS, 3)), dma((CHUNKS, 3)), dma((CHUNKS,)),
            dma((CHUNKS, 2)), dma((CHUNKS, 2)), dma((CHUNKS, 2, 3)), dma((CHUNKS, 2, 3)), dma((CHUNKS, 2)), dma((CHUNKS, 2)),
            dma((CHUNKS, 4)), dma((CHUNKS, 4)), dma((CHUNKS,)), dma((CHUNKS,)),
            dma((GROUPS, 3)), dma((GROUPS, 3)), dma((GROUPS, 2, RING)), dma((GROUPS, 2, RING)), dma((GROUPS, 2, 2)), dma((GROUPS, 2, 2)),
            dma((2, 3, CHUNKS)), dma((2, 3, CHUNKS)), dma((2, 2, CHUNKS)), dma((2, 2, CHUNKS)),
        ],
        compiler_params=pltpu.CompilerParams(
            collective_id=0, has_side_effects=True, vmem_limit_bytes=56 * 2**20
        ),
        name="gram",
    )(slab_start, routes.T, tokens)
    return result[None]


def solution(mesh):
    placed = (P(("expert", "dp"), None), P(("expert", "dp"), None), P())
    return jax.shard_map(
        shards, mesh=mesh, in_specs=placed, out_specs=P("expert", None, "dp"), check_vma=False
    )
```

```python
import jax
import jax.numpy as jnp
from jax import lax
from jax.experimental import pallas as pl
from jax.experimental.pallas import tpu as pltpu
from jax.sharding import PartitionSpec as P

MESH = pl.DeviceIdType.MESH
SLAB = 448
CAP = 40
PAIR = 2 * CAP
FULL = 3 * PAIR
TAIL = 48
RING = 4
TOK = 128
WIDTH = 7168
BLOCK = WIDTH // RING
CHUNK = 256
CHUNKS = BLOCK // CHUNK
PLACES = RING * RING
GROUPS = 4
OFFSETS = (2, 1, 3, 0)
SCALE_ROWS = 112
HALF = SLAB // 2
SPAN = 640

CODES = {
    "U": 0, "V": 28, "XO": 42, "XA": 49, "XB": 56, "C": 63, "Z": 70, "P": 77, "WZ": 81, "WZF": 85, "EXP": 89, "S": 93,
}
SCHEDULE = (
    "XO1", "XO2", "XO0", "Z5", "XA0", "S0", "P0", "P2", "XB0", "WZ0", "XA1", "WZ2", "WZF0", "C0", "P1", "XA2",
    "XB1", "WZ1", "WZF2", "EXP0", "U00", "XB2", "XO5", "P3", "C1", "WZF1", "Z4", "XO4", "XO3", "XA5", "C2", "U01",
    "EXP2", "U02", "U21", "EXP1", "U11", "XA4", "V11", "V01", "Z3", "U10", "V00", "U20", "XB5", "Z6", "U22", "XB4",
    "U12", "XO6", "V10", "C5", "V12", "WZ3", "V02", "XA3", "XA6", "C4", "U05", "U25", "U04", "U15", "WZF3", "U14",
    "XB3", "U24", "V05", "V04", "XB6", "V15", "EXP3", "V14", "C3", "U34", "U35", "C6", "U03", "U13", "U06", "U23",
    "U33", "V03", "V13", "U32", "U16", "U26", "V16", "V06", "U30", "U36", "U31",
)


def plan():
    codes = []
    for item in SCHEDULE:
        name = item.rstrip("0123456789")
        digits = item[len(name):]
        value = int(digits[0]) * CHUNKS + int(digits[1]) if len(digits) == 2 else int(digits)
        codes.append(CODES[name] + value)
    padded = codes + [0] * (-len(codes) % 4)
    words = [sum(padded[at + i] * 128 ** i for i in range(4)) for at in range(0, len(padded), 4)]
    return words, len(codes)


def finish_word():
    last = {}
    for at, item in enumerate(SCHEDULE):
        if item[0] == "V" or item[:2] in ("U1", "U2"):
            last[int(item[2])] = at
    return sum(k * 16 ** place for place, k in enumerate(sorted(last, key=last.get)))


def looked_up(words, step):
    word = jnp.int32(words[0])
    for at in range(1, len(words)):
        word = jnp.where(step // 4 == at, jnp.int32(words[at]), word)
    return lax.shift_right_logical(word, 7 * (step % 4)) % 128


def offset_of(group):
    value = jnp.int32(OFFSETS[0])
    for index in range(1, GROUPS):
        value = jnp.where(group == index, jnp.int32(OFFSETS[index]), value)
    return value


def gram_kernel(
    start_ref, routes_ref, tok_ref, out_ref,
    both, listed, slots, packed, win, chosen, wide, cols, near, part, kept, quant, scale, got_q, got_s, hits,
    pair_s, pair_r, own_s, z_s, z_r, zl_s, xo_s, xo_r, xa_s, xa_r, xb_s, xb_r, ca_s, ca_r, c_s, c_r,
    wx_s, wx_r, wz_s, wz_r, wf_s, wf_r, q_s, q_r, f_s, f_r,
):
    expert = lax.axis_index("expert")
    z = lax.axis_index("dp")
    core = expert % 2
    x = (expert // 2) % RING
    y = expert // (2 * RING)

    def device(dy=0, dx=0, dz=0, dc=0):
        ey, ex, ec = (y + dy) % RING, (x + dx) % RING, (core + dc) % 2
        return ((ey * RING + ex) * 2 + ec, (z + dz) % RING)

    def remote(src, dst, send, recv, to):
        return pltpu.make_async_remote_copy(
            src_ref=src, dst_ref=dst, send_sem=send, recv_sem=recv, device_id=to, device_id_type=MESH
        )

    def pair_copies():
        return (
            remote(routes_ref, listed.at[core], pair_s.at[0], pair_r.at[0], device(dc=1)),
            remote(tok_ref, both.at[pl.ds(core * TOK, TOK)], pair_s.at[1], pair_r.at[1], device(dc=1)),
        )

    def own_copy():
        return pltpu.make_async_copy(tok_ref, both.at[pl.ds(core * TOK, TOK)], own_s)

    def z_copy(k, d):
        first = pl.multiple_of(((z + d) % RING) * BLOCK + k * CHUNK, 128)
        return remote(
            tok_ref.at[:, pl.ds(first, CHUNK)], cols.at[k, core, x, z], z_s.at[k, d - 1], z_r.at[k, d - 1], device(dz=d)
        )

    def z_local(k):
        first = pl.multiple_of(z * BLOCK + k * CHUNK, 128)
        return pltpu.make_async_copy(tok_ref.at[:, pl.ds(first, CHUNK)], cols.at[k, core, x, z], zl_s.at[k])

    def xo_copy(k, way):
        here = cols.at[k, core, x, z]
        return remote(here, here, xo_s.at[k, way], xo_r.at[k, way], device(dx=1 if way == 0 else 3))

    def xa_copy(k, way, d):
        here = cols.at[k, core, x, (z + RING - d) % RING]
        return remote(here, here, xa_s.at[k, way, d - 1], xa_r.at[k, way, d - 1], device(dx=1 if way == 0 else 3))

    def xb_copy(k, way):
        origin = (x + (3 if way == 0 else 1)) % RING
        here = cols.at[k, core, origin, pl.ds(2 * way, 2)]
        return remote(here, here, xb_s.at[k, way], xb_r.at[k, way], device(dx=1 if way == 0 else 3))

    def ca_copy(k, d):
        here = cols.at[k, core, (x + d) % RING]
        return remote(here, here, ca_s.at[k, d % RING], ca_r.at[k, d % RING], device(dc=1))

    def c_copy(k):
        here = cols.at[k, core, (x + 2) % RING]
        return remote(here, here, c_s.at[k], c_r.at[k], device(dc=1))

    def wx_copy(g, d):
        return remote(
            packed.at[g * RING + d], win.at[g, z, x], wx_s.at[g, d - 1], wx_r.at[g, d - 1], device(dx=d)
        )

    def wz_copy(g, way, d):
        here = win.at[g, z, (x + RING - d) % RING]
        return remote(here, here, wz_s.at[g, way, d], wz_r.at[g, way, d], device(dz=1 if way == 0 else 3))

    def wf_copy(g, way, d):
        here = win.at[g, (z + (3 if way == 0 else 1)) % RING, (x + RING - d) % RING]
        return remote(here, here, wf_s.at[g, way, d % 2], wf_r.at[g, way, d % 2], device(dz=1 if way == 0 else 3))

    def sum_copies(way, slot, k):
        to = device(dy=1 if way == 0 else 3)
        values = remote(quant.at[way, slot, k], got_q.at[way, slot, k], q_s.at[way, slot, k], q_r.at[way, slot, k], to)
        if slot == 1:
            return (values,)
        at = slot // 2
        return (values, remote(scale.at[way, at, k], got_s.at[way, at, k], f_s.at[way, at, k], f_r.at[way, at, k], to))

    for k in range(CHUNKS):
        z_local(k).start()
    own_copy().start()

    barrier = pltpu.get_barrier_semaphore()
    peers = [device(dc=1), device(dy=1), device(dy=3)]
    peers += [device(dx=d) for d in (1, 2, 3)] + [device(dz=d) for d in (1, 2, 3)]
    for peer in peers:
        pl.semaphore_signal(barrier, inc=1, device_id=peer, device_id_type=MESH)
    pl.semaphore_wait(barrier, len(peers))

    def send_z(k):
        for d in (1, 3, 2):
            z_copy(k, d).start()

    for copy in pair_copies():
        copy.start()
    for k in range(3):
        send_z(jnp.int32(k))
    listed[core] = routes_ref[...]

    def take_xo(k):
        z_local(k).wait()
        for way in (0, 1):
            xo_copy(k, way).start()

    def take_xa(k):
        for d in (1, 3, 2):
            z_copy(k, d).wait_recv()
            for way in (0, 1):
                xa_copy(k, way, d).start()

    def take_xb(k):
        for way in (0, 1):
            xo_copy(k, way).wait_recv()
            for d in (1, 2, 3):
                xa_copy(k, way, d).wait_recv()
            xb_copy(k, way).start()
        for d in (0, 1, 3):
            ca_copy(k, d).start()

    def take_c(k):
        for way in (0, 1):
            xb_copy(k, way).wait_recv()
        c_copy(k).start()

    def find_slots(_):
        for copy in pair_copies():
            copy.wait_recv()
        own_copy().wait()
        named = jnp.concatenate([listed[0], listed[1]], axis=1)
        row = lax.broadcasted_iota(jnp.int32, (GROUPS * RING, 2 * TOK), 0)
        group, step = row // RING, row % RING
        away = jnp.where(group == 0, OFFSETS[0], jnp.where(group == 1, OFFSETS[1], jnp.where(group == 2, OFFSETS[2], OFFSETS[3])))
        label = (((y + away) % RING) * RING + (x + step) % RING) * 2 + core
        hit = jnp.zeros((GROUPS * RING, 2 * TOK), jnp.float32)
        for choice in range(named.shape[0]):
            hit += jnp.where(named[choice:choice + 1, :] == label, 1.0, 0.0)
        before = lax.broadcasted_iota(jnp.int32, (2 * TOK, 2 * TOK), 0) < lax.broadcasted_iota(
            jnp.int32, (2 * TOK, 2 * TOK), 1
        )
        rank = jnp.dot(
            hit.astype(jnp.bfloat16), jnp.where(before, 1.0, 0.0).astype(jnp.bfloat16), preferred_element_type=jnp.float32
        )
        slots[...] = jnp.where(hit > 0.0, rank, -1.0)

    def take_p(g):
        slot = lax.broadcasted_iota(jnp.int32, (PAIR, 2 * TOK), 0).astype(jnp.float32)
        source = lax.broadcasted_iota(jnp.int32, (SPAN, 512), 0)
        target = lax.broadcasted_iota(jnp.int32, (SPAN, 512), 1)
        for d in (2, 1, 3, 0):
            row = g * RING + d
            taken = jnp.where(slots[pl.ds(row, 1), :] == slot, 1.0, 0.0).astype(jnp.bfloat16)
            label = (((y + offset_of(g)) % RING) * RING + (x + d) % RING) * 2 + core
            start = start_ref[label]
            tile = jnp.minimum(lax.div(start, jnp.int32(128)), (WIDTH - SPAN) // 128)
            shift = start - tile * 128
            first = tile * 128
            rows = both[:, pl.ds(first, SPAN)]
            picked = jnp.dot(taken, rows, preferred_element_type=jnp.float32)
            moved = jnp.where(source == target + shift, 1.0, 0.0).astype(jnp.bfloat16)
            picked = jnp.dot(picked.astype(jnp.bfloat16), moved, preferred_element_type=jnp.float32)
            rest = picked[:, 384:SLAB]
            seat = slots[pl.ds(row, 1), :]
            seats = [seat[:, 64 * part:64 * part + 64] for part in range(4)] + [jnp.zeros((12, 64), jnp.float32)]
            tail = jnp.concatenate([rest[:TAIL], jnp.concatenate([rest[TAIL:]] + seats, axis=0)], axis=1)
            blocks = [picked[:, 128 * tile:128 * tile + 128] for tile in range(3)] + [tail]
            value = jnp.concatenate(blocks, axis=0).astype(jnp.bfloat16)
            if d == 0:
                win[g, z, x] = value
                for way in (0, 1):
                    wz_copy(g, way, 0).start()
            else:
                packed[row] = value
                wx_copy(g, d).start()

    def take_wz(g):
        for d in (1, 3, 2):
            wx_copy(g, d).wait_recv()
            for way in (0, 1):
                wz_copy(g, way, d).start()

    def take_wzf(g):
        for way in (0, 1):
            for d in (2 * way, 2 * way + 1):
                wz_copy(g, way, d).wait_recv()
                wf_copy(g, way, d).start()

    def take_exp(g):
        for way in (0, 1):
            for d in (2 * way, 2 * way + 1):
                wz_copy(g, 1 - way, d).wait_recv()
                wf_copy(g, way, d).wait_recv()
        slot = lax.broadcasted_iota(jnp.int32, (PAIR, 2 * TOK), 0).astype(jnp.float32)
        low = lax.broadcasted_iota(jnp.int32, (1, 128), 1) < 64
        total = jnp.zeros((1, 2 * TOK), jnp.float32)
        seats = win[g, :, :, FULL + PAIR - TAIL:, :].reshape(PLACES * 16, 128).astype(jnp.float32)[:, 64:]
        seats = jnp.concatenate([seats, seats], axis=1)
        for place in range(PLACES):
            rows = [seats[16 * place + part:16 * place + part + 1] for part in range(4)]
            seat = jnp.concatenate([jnp.where(low, rows[0], rows[1]), jnp.where(low, rows[2], rows[3])], axis=1)
            chosen[g, place] = jnp.where(seat == slot, 1.0, 0.0).astype(jnp.bfloat16)
            total += jnp.where(seat >= 0.0, 1.0, 0.0)
        hits[g] = total[:, :TOK] + total[:, TOK:]
        split = PLACES * TAIL
        for tile in range(3):
            at = tile * PAIR
            block = win[g, :, :, at:at + TAIL, :].reshape(split, 128)
            wide[g, tile * 128:(tile + 1) * 128, :split] = block.T
            block = win[g, :, :, at + TAIL:at + PAIR, :].reshape(PLACES * (PAIR - TAIL), 128)
            wide[g, tile * 128:(tile + 1) * 128, split:] = block.T
        wide[g, 384:, :split] = win[g, :, :, FULL:, :].reshape(split, 128).T[:64]
        wide[g, 384:, split:] = win[g, :, :, FULL:FULL + PAIR - TAIL, :].reshape(PLACES * (PAIR - TAIL), 128).T[64:]

    def scale_row(slot, piece):
        return (slot + 1) // 2, pl.ds(piece + (2 if slot == 1 else 0), 1)

    def restored(way, slot, k, piece):
        block = got_q[way, slot, k, pl.ds(piece * SCALE_ROWS, SCALE_ROWS), :]
        at, row = scale_row(slot, piece)
        factor = got_s[way, at, k, row, :]
        return block.astype(jnp.int32).astype(jnp.float32) * jnp.concatenate([factor, factor], axis=1)

    def send_sum(way, slot, k, pieces, count):
        for piece, block in enumerate(pieces):
            most = jnp.max(jnp.abs(block), axis=0, keepdims=True)
            most = jnp.maximum(most[:, :128], most[:, 128:])
            factor = jnp.where(most > 0.0, 32767.0 / jnp.where(most > 0.0, most, 1.0), 0.0)
            factor = jnp.concatenate([factor, factor], axis=1)
            rows = pl.ds(piece * SCALE_ROWS, SCALE_ROWS)
            quant[way, slot, k, rows, :] = jnp.round(block * factor).astype(jnp.int32).astype(jnp.int16)
            at, row = scale_row(slot, piece)
            scale[way, at, k, row, :] = most * (1.0 / 32767.0)
        if count is not None:
            scale[way, slot // 2, k, pl.ds(7, 1), :] = count
        for copy in sum_copies(way, slot, k):
            copy.start()

    def take_u(unit):
        g, k = unit // CHUNKS, unit % CHUNKS

        @pl.when(g == 0)
        def _():
            for d in (0, 1, 3):
                ca_copy(k, d).wait_recv()
            c_copy(k).wait_recv()

        for place in range(PLACES):
            from_x, from_z = place % RING, place // RING
            tokens = jnp.concatenate([cols[k, 0, from_x, from_z], cols[k, 1, from_x, from_z]], axis=0)
            picked = jnp.dot(chosen[g, place], tokens, preferred_element_type=jnp.float32).astype(jnp.bfloat16)
            near[pl.ds(place * TAIL, TAIL), :] = picked[:TAIL]
            near[pl.ds(PLACES * TAIL + place * (PAIR - TAIL), PAIR - TAIL), :] = picked[TAIL:]
        part[...] = jnp.dot(wide[g], near[...], preferred_element_type=jnp.float32)

        def pieces(half):
            first = half * HALF
            return [part[first + SCALE_ROWS * piece:first + SCALE_ROWS * (piece + 1), :] for piece in range(2)]

        @pl.when(g == 0)
        def _():
            for way in (0, 1):
                send_sum(way, 0, k, pieces(way), hits[g])

        for way in (0, 1):
            @pl.when(g == 1 + way)
            def _():
                send_sum(way, 1, k, pieces(1 - way), None)
                kept[way, k] = part[way * HALF:(way + 1) * HALF, :]

        @pl.when(g == 3)
        def _():
            out_ref[:, pl.ds(pl.multiple_of(k * CHUNK, 128), CHUNK)] = part[...]

    def take_v(unit):
        k = unit % CHUNKS
        for way in (0, 1):
            @pl.when(unit // CHUNKS == way)
            def _():
                for copy in sum_copies(way, 0, k):
                    copy.wait_recv()
                pieces = [
                    kept[way, k, pl.ds(piece * SCALE_ROWS, SCALE_ROWS), :] + restored(way, 0, k, piece)
                    for piece in range(2)
                ]
                below = got_s[way, 0, k, pl.ds(7, 1), :]
                send_sum(way, 2, k, pieces, hits[1] + below if way == 0 else hits[2])

    actions = {
        "S": find_slots, "P": take_p, "XO": take_xo, "XA": take_xa, "XB": take_xb, "Z": send_z, "WZ": take_wz,
        "WZF": take_wzf, "C": take_c, "EXP": take_exp, "U": take_u, "V": take_v,
    }
    words, length = plan()

    def one_step(step, carry):
        code = looked_up(words, step)

        def among(names):
            if len(names) == 1:
                actions[names[0]](code - CODES[names[0]])
                return
            middle = len(names) // 2
            low = code < CODES[names[middle]]
            pl.when(low)(lambda: among(names[:middle]))
            pl.when(jnp.logical_not(low))(lambda: among(names[middle:]))

        among(list(CODES))
        return carry

    lax.fori_loop(0, length, one_step, 0)

    def drain(k, carry):
        for d in (1, 2, 3):
            z_copy(k, d).wait_send()
            for way in (0, 1):
                xa_copy(k, way, d).wait_send()
        for d in (0, 1, 3):
            ca_copy(k, d).wait_send()
        c_copy(k).wait_send()
        for way in (0, 1):
            xo_copy(k, way).wait_send()
            xb_copy(k, way).wait_send()
        return carry

    def drain_windows(g, carry):
        for d in (1, 2, 3):
            wx_copy(g, d).wait_send()
        for way in (0, 1):
            for d in range(RING):
                wz_copy(g, way, d).wait_send()
            for d in (2 * way, 2 * way + 1):
                wf_copy(g, way, d).wait_send()
        return carry

    for copy in pair_copies():
        copy.wait_send()
    lax.fori_loop(0, CHUNKS, drain, 0)
    lax.fori_loop(0, GROUPS, drain_windows, 0)

    def finish(place, carry):
        k = lax.shift_right_logical(jnp.int32(finish_word()), 4 * place) % 16
        for way in (0, 1):
            for slot in range(3):
                for copy in sum_copies(way, slot, k):
                    copy.wait_send()
        for way in (0, 1):
            for slot in (1, 2):
                for copy in sum_copies(way, slot, k):
                    copy.wait_recv()
        count = hits[3] + got_s[0, 1, k, pl.ds(7, 1), :] + got_s[1, 1, k, pl.ds(7, 1), :]
        inverse = 1.0 / jnp.sum(count, axis=1, keepdims=True)
        at = pl.ds(pl.multiple_of(k * CHUNK, 128), CHUNK)
        for half in (0, 1):
            for piece in (0, 1):
                rows = pl.ds(half * HALF + piece * SCALE_ROWS, SCALE_ROWS)
                total = out_ref[rows, at] + restored(half, 2, k, piece) + restored(1 - half, 1, k, piece)
                out_ref[rows, at] = total * inverse
        return carry

    lax.fori_loop(0, CHUNKS, finish, 0)


def shards(tokens, routes, slab_start):
    dma = pltpu.SemaphoreType.DMA
    bf16, f32, i16 = jnp.bfloat16, jnp.float32, jnp.int16
    result = pl.pallas_call(
        gram_kernel,
        out_shape=pltpu.VMEM((SLAB, BLOCK), f32),
        in_specs=[
            pl.BlockSpec(memory_space=pltpu.SMEM),
            pl.BlockSpec(memory_space=pltpu.VMEM),
            pl.BlockSpec(memory_space=pl.ANY),
        ],
        out_specs=pl.BlockSpec(memory_space=pltpu.VMEM),
        scratch_shapes=[
            pltpu.VMEM((2 * TOK, WIDTH), bf16),
            pltpu.VMEM((2, 8, TOK), jnp.int32),
            pltpu.VMEM((GROUPS * RING, 2 * TOK), f32),
            pltpu.VMEM((GROUPS * RING, FULL + TAIL, 128), bf16),
            pltpu.VMEM((GROUPS, RING, RING, FULL + TAIL, 128), bf16),
            pltpu.VMEM((GROUPS, PLACES, PAIR, 2 * TOK), bf16),
            pltpu.VMEM((GROUPS, SLAB, PLACES * PAIR), bf16),
            pltpu.VMEM((CHUNKS, 2, RING, RING, TOK, CHUNK), bf16),
            pltpu.VMEM((PLACES * PAIR, CHUNK), bf16),
            pltpu.VMEM((SLAB, CHUNK), f32),
            pltpu.VMEM((2, CHUNKS, HALF, CHUNK), f32),
            pltpu.VMEM((2, 3, CHUNKS, HALF, CHUNK), i16),
            pltpu.VMEM((2, 2, CHUNKS, 8, 128), f32),
            pltpu.VMEM((2, 3, CHUNKS, HALF, CHUNK), i16),
            pltpu.VMEM((2, 2, CHUNKS, 8, 128), f32),
            pltpu.VMEM((GROUPS, 1, TOK), f32),
            dma((2,)), dma((2,)), dma(()),
            dma((CHUNKS, 3)), dma((CHUNKS, 3)), dma((CHUNKS,)),
            dma((CHUNKS, 2)), dma((CHUNKS, 2)), dma((CHUNKS, 2, 3)), dma((CHUNKS, 2, 3)), dma((CHUNKS, 2)), dma((CHUNKS, 2)),
            dma((CHUNKS, 4)), dma((CHUNKS, 4)), dma((CHUNKS,)), dma((CHUNKS,)),
            dma((GROUPS, 3)), dma((GROUPS, 3)), dma((GROUPS, 2, RING)), dma((GROUPS, 2, RING)), dma((GROUPS, 2, 2)), dma((GROUPS, 2, 2)),
            dma((2, 3, CHUNKS)), dma((2, 3, CHUNKS)), dma((2, 2, CHUNKS)), dma((2, 2, CHUNKS)),
        ],
        compiler_params=pltpu.CompilerParams(
            collective_id=0, has_side_effects=True, vmem_limit_bytes=56 * 2**20
        ),
        name="gram",
    )(slab_start, routes.T, tokens)
    return result[None]


def solution(mesh):
    placed = (P(("expert", "dp"), None), P(("expert", "dp"), None), P())
    return jax.shard_map(
        shards, mesh=mesh, in_specs=placed, out_specs=P("expert", None, "dp"), check_vma=False
    )
```

```python
import jax
import jax.numpy as jnp
from jax import lax
from jax.experimental import pallas as pl
from jax.experimental.pallas import tpu as pltpu
from jax.sharding import PartitionSpec as P

MESH = pl.DeviceIdType.MESH
SLAB = 448
CAP = 40
PAIR = 2 * CAP
FULL = 3 * PAIR
TAIL = 48
RING = 4
TOK = 128
WIDTH = 7168
BLOCK = WIDTH // RING
CHUNK = 256
CHUNKS = BLOCK // CHUNK
PLACES = RING * RING
GROUPS = 4
OFFSETS = (2, 1, 3, 0)
SCALE_ROWS = 112
HALF = SLAB // 2
SPAN = 640

CODES = {
    "U": 0, "V": 28, "XO": 42, "XA": 49, "XB": 56, "C": 63, "Z": 70, "P": 77, "WZ": 81, "WZF": 85, "EXP": 89, "S": 93,
}
SCHEDULE = (
    "XO1", "XO0", "XO4", "Z4", "XA0", "S0", "P0", "P1", "XA1", "P2", "WZ0", "XB0", "XA4", "WZ1", "WZF0", "C0",
    "WZ2", "WZF1", "XB1", "EXP0", "XB4", "XO2", "XA2", "XO6", "U00", "C1", "WZF2", "P3", "C4", "U01", "EXP1", "U10",
    "U04", "EXP2", "Z5", "U21", "XB2", "V00", "XO5", "U20", "Z6", "V11", "U14", "XA5", "U24", "V04", "C2", "U11",
    "XA6", "V01", "Z3", "WZ3", "V10", "U02", "XB5", "V14", "U22", "U12", "XB6", "XO3", "V12", "C5", "XA3", "WZF3",
    "V02", "U05", "C6", "U15", "U25", "EXP3", "U06", "XB3", "V15", "U36", "V05", "U16", "U26", "C3", "V06", "U32",
    "V16", "U30", "U03", "U23", "U13", "U35", "U33", "U34", "V03", "V13", "U31",
)


def plan():
    codes = []
    for item in SCHEDULE:
        name = item.rstrip("0123456789")
        digits = item[len(name):]
        value = int(digits[0]) * CHUNKS + int(digits[1]) if len(digits) == 2 else int(digits)
        codes.append(CODES[name] + value)
    padded = codes + [0] * (-len(codes) % 4)
    words = [sum(padded[at + i] * 128 ** i for i in range(4)) for at in range(0, len(padded), 4)]
    return words, len(codes)


def finish_word():
    last = {}
    for at, item in enumerate(SCHEDULE):
        if item[0] == "V" or item[:2] in ("U1", "U2"):
            last[int(item[2])] = at
    return sum(k * 16 ** place for place, k in enumerate(sorted(last, key=last.get)))


def looked_up(words, step):
    word = jnp.int32(words[0])
    for at in range(1, len(words)):
        word = jnp.where(step // 4 == at, jnp.int32(words[at]), word)
    return lax.shift_right_logical(word, 7 * (step % 4)) % 128


def offset_of(group):
    value = jnp.int32(OFFSETS[0])
    for index in range(1, GROUPS):
        value = jnp.where(group == index, jnp.int32(OFFSETS[index]), value)
    return value


def gram_kernel(
    start_ref, routes_ref, tok_ref, out_ref,
    both, listed, slots, packed, win, chosen, wide, cols, near, part, kept, quant, scale, got_q, got_s, hits,
    pair_s, pair_r, own_s, z_s, z_r, zl_s, xo_s, xo_r, xa_s, xa_r, xb_s, xb_r, ca_s, ca_r, c_s, c_r,
    wx_s, wx_r, wz_s, wz_r, wf_s, wf_r, q_s, q_r, f_s, f_r,
):
    expert = lax.axis_index("expert")
    z = lax.axis_index("dp")
    core = expert % 2
    x = (expert // 2) % RING
    y = expert // (2 * RING)

    def device(dy=0, dx=0, dz=0, dc=0):
        ey, ex, ec = (y + dy) % RING, (x + dx) % RING, (core + dc) % 2
        return ((ey * RING + ex) * 2 + ec, (z + dz) % RING)

    def remote(src, dst, send, recv, to):
        return pltpu.make_async_remote_copy(
            src_ref=src, dst_ref=dst, send_sem=send, recv_sem=recv, device_id=to, device_id_type=MESH
        )

    def pair_copies():
        return (
            remote(routes_ref, listed.at[core], pair_s.at[0], pair_r.at[0], device(dc=1)),
            remote(tok_ref, both.at[pl.ds(core * TOK, TOK)], pair_s.at[1], pair_r.at[1], device(dc=1)),
        )

    def own_copy():
        return pltpu.make_async_copy(tok_ref, both.at[pl.ds(core * TOK, TOK)], own_s)

    def z_copy(k, d):
        first = pl.multiple_of(((z + d) % RING) * BLOCK + k * CHUNK, 128)
        return remote(
            tok_ref.at[:, pl.ds(first, CHUNK)], cols.at[k, core, x, z], z_s.at[k, d - 1], z_r.at[k, d - 1], device(dz=d)
        )

    def z_local(k):
        first = pl.multiple_of(z * BLOCK + k * CHUNK, 128)
        return pltpu.make_async_copy(tok_ref.at[:, pl.ds(first, CHUNK)], cols.at[k, core, x, z], zl_s.at[k])

    def xo_copy(k, way):
        here = cols.at[k, core, x, z]
        return remote(here, here, xo_s.at[k, way], xo_r.at[k, way], device(dx=1 if way == 0 else 3))

    def xa_copy(k, way, d):
        here = cols.at[k, core, x, (z + RING - d) % RING]
        return remote(here, here, xa_s.at[k, way, d - 1], xa_r.at[k, way, d - 1], device(dx=1 if way == 0 else 3))

    def xb_copy(k, way):
        origin = (x + (3 if way == 0 else 1)) % RING
        here = cols.at[k, core, origin, pl.ds(2 * way, 2)]
        return remote(here, here, xb_s.at[k, way], xb_r.at[k, way], device(dx=1 if way == 0 else 3))

    def ca_copy(k, d):
        here = cols.at[k, core, (x + d) % RING]
        return remote(here, here, ca_s.at[k, d % RING], ca_r.at[k, d % RING], device(dc=1))

    def c_copy(k):
        here = cols.at[k, core, (x + 2) % RING]
        return remote(here, here, c_s.at[k], c_r.at[k], device(dc=1))

    def wx_copy(g, d):
        return remote(
            packed.at[g * RING + d], win.at[g, z, x], wx_s.at[g, d - 1], wx_r.at[g, d - 1], device(dx=d)
        )

    def wz_copy(g, way, d):
        here = win.at[g, z, (x + RING - d) % RING]
        return remote(here, here, wz_s.at[g, way, d], wz_r.at[g, way, d], device(dz=1 if way == 0 else 3))

    def wf_copy(g, way, d):
        here = win.at[g, (z + (3 if way == 0 else 1)) % RING, (x + RING - d) % RING]
        return remote(here, here, wf_s.at[g, way, d % 2], wf_r.at[g, way, d % 2], device(dz=1 if way == 0 else 3))

    def sum_copies(way, slot, k):
        to = device(dy=1 if way == 0 else 3)
        values = remote(quant.at[way, slot, k], got_q.at[way, slot, k], q_s.at[way, slot, k], q_r.at[way, slot, k], to)
        if slot == 1:
            return (values,)
        at = slot // 2
        return (values, remote(scale.at[way, at, k], got_s.at[way, at, k], f_s.at[way, at, k], f_r.at[way, at, k], to))

    for k in range(CHUNKS):
        z_local(k).start()
    own_copy().start()

    barrier = pltpu.get_barrier_semaphore()
    peers = [device(dc=1), device(dy=1), device(dy=3)]
    peers += [device(dx=d) for d in (1, 2, 3)] + [device(dz=d) for d in (1, 2, 3)]
    for peer in peers:
        pl.semaphore_signal(barrier, inc=1, device_id=peer, device_id_type=MESH)
    pl.semaphore_wait(barrier, len(peers))

    def send_z(k):
        for d in (1, 3, 2):
            z_copy(k, d).start()

    for copy in pair_copies():
        copy.start()
    for k in range(3):
        send_z(jnp.int32(k))
    listed[core] = routes_ref[...]

    def take_xo(k):
        z_local(k).wait()
        for way in (0, 1):
            xo_copy(k, way).start()

    def take_xa(k):
        for d in (1, 3, 2):
            z_copy(k, d).wait_recv()
            for way in (0, 1):
                xa_copy(k, way, d).start()

    def take_xb(k):
        for way in (0, 1):
            xo_copy(k, way).wait_recv()
            for d in (1, 2, 3):
                xa_copy(k, way, d).wait_recv()
            xb_copy(k, way).start()
        for d in (0, 1, 3):
            ca_copy(k, d).start()

    def take_c(k):
        for way in (0, 1):
            xb_copy(k, way).wait_recv()
        c_copy(k).start()

    def find_slots(_):
        for copy in pair_copies():
            copy.wait_recv()
        own_copy().wait()
        named = jnp.concatenate([listed[0], listed[1]], axis=1)
        row = lax.broadcasted_iota(jnp.int32, (GROUPS * RING, 2 * TOK), 0)
        group, step = row // RING, row % RING
        away = jnp.where(group == 0, OFFSETS[0], jnp.where(group == 1, OFFSETS[1], jnp.where(group == 2, OFFSETS[2], OFFSETS[3])))
        label = (((y + away) % RING) * RING + (x + step) % RING) * 2 + core
        hit = jnp.zeros((GROUPS * RING, 2 * TOK), jnp.float32)
        for choice in range(named.shape[0]):
            hit += jnp.where(named[choice:choice + 1, :] == label, 1.0, 0.0)
        before = lax.broadcasted_iota(jnp.int32, (2 * TOK, 2 * TOK), 0) < lax.broadcasted_iota(
            jnp.int32, (2 * TOK, 2 * TOK), 1
        )
        rank = jnp.dot(
            hit.astype(jnp.bfloat16), jnp.where(before, 1.0, 0.0).astype(jnp.bfloat16), preferred_element_type=jnp.float32
        )
        slots[...] = jnp.where(hit > 0.0, rank, -1.0)

    def take_p(g):
        slot = lax.broadcasted_iota(jnp.int32, (PAIR, 2 * TOK), 0).astype(jnp.float32)
        source = lax.broadcasted_iota(jnp.int32, (SPAN, SLAB), 0)
        target = lax.broadcasted_iota(jnp.int32, (SPAN, SLAB), 1)
        for d in (2, 1, 3, 0):
            row = g * RING + d
            taken = jnp.where(slots[pl.ds(row, 1), :] == slot, 1.0, 0.0).astype(jnp.bfloat16)
            label = (((y + offset_of(g)) % RING) * RING + (x + d) % RING) * 2 + core
            start = start_ref[label]
            tile = jnp.minimum(lax.div(start, jnp.int32(128)), (WIDTH - SPAN) // 128)
            shift = start - tile * 128
            first = tile * 128
            rows = both[:, pl.ds(first, SPAN)]
            picked = jnp.dot(taken, rows, preferred_element_type=jnp.float32)
            moved = jnp.where(source == target + shift, 1.0, 0.0).astype(jnp.bfloat16)
            picked = jnp.dot(picked.astype(jnp.bfloat16), moved, preferred_element_type=jnp.float32)
            rest = picked[:, 384:SLAB]
            seat = slots[pl.ds(row, 1), :]
            seats = [seat[:, 64 * part:64 * part + 64] for part in range(4)] + [jnp.zeros((12, 64), jnp.float32)]
            tail = jnp.concatenate([rest[:TAIL], jnp.concatenate([rest[TAIL:]] + seats, axis=0)], axis=1)
            blocks = [picked[:, 128 * tile:128 * tile + 128] for tile in range(3)] + [tail]
            value = jnp.concatenate(blocks, axis=0).astype(jnp.bfloat16)
            if d == 0:
                win[g, z, x] = value
                for way in (0, 1):
                    wz_copy(g, way, 0).start()
            else:
                packed[row] = value
                wx_copy(g, d).start()

    def take_wz(g):
        for d in (1, 3, 2):
            wx_copy(g, d).wait_recv()
            for way in (0, 1):
                wz_copy(g, way, d).start()

    def take_wzf(g):
        for way in (0, 1):
            for d in (2 * way, 2 * way + 1):
                wz_copy(g, way, d).wait_recv()
                wf_copy(g, way, d).start()

    def take_exp(g):
        for way in (0, 1):
            for d in (2 * way, 2 * way + 1):
                wz_copy(g, 1 - way, d).wait_recv()
                wf_copy(g, way, d).wait_recv()
        slot = lax.broadcasted_iota(jnp.int32, (PAIR, 2 * TOK), 0).astype(jnp.float32)
        low = lax.broadcasted_iota(jnp.int32, (1, 128), 1) < 64
        total = jnp.zeros((1, 2 * TOK), jnp.float32)
        seats = win[g, :, :, FULL + PAIR - TAIL:, :].reshape(PLACES * 16, 128).astype(jnp.float32)[:, 64:]
        seats = jnp.concatenate([seats, seats], axis=1)
        for place in range(PLACES):
            rows = [seats[16 * place + part:16 * place + part + 1] for part in range(4)]
            seat = jnp.concatenate([jnp.where(low, rows[0], rows[1]), jnp.where(low, rows[2], rows[3])], axis=1)
            chosen[g, place] = jnp.where(seat == slot, 1.0, 0.0).astype(jnp.bfloat16)
            total += jnp.where(seat >= 0.0, 1.0, 0.0)
        hits[g] = total[:, :TOK] + total[:, TOK:]
        split = PLACES * TAIL
        for tile in range(3):
            at = tile * PAIR
            block = win[g, :, :, at:at + TAIL, :].reshape(split, 128)
            wide[g, tile * 128:(tile + 1) * 128, :split] = block.T
            block = win[g, :, :, at + TAIL:at + PAIR, :].reshape(PLACES * (PAIR - TAIL), 128)
            wide[g, tile * 128:(tile + 1) * 128, split:] = block.T
        wide[g, 384:, :split] = win[g, :, :, FULL:, :].reshape(split, 128).T[:64]
        wide[g, 384:, split:] = win[g, :, :, FULL:FULL + PAIR - TAIL, :].reshape(PLACES * (PAIR - TAIL), 128).T[64:]

    def scale_row(slot, piece):
        return (slot + 1) // 2, pl.ds(piece + (2 if slot == 1 else 0), 1)

    def restored(way, slot, k, piece):
        block = got_q[way, slot, k, pl.ds(piece * SCALE_ROWS, SCALE_ROWS), :]
        at, row = scale_row(slot, piece)
        factor = got_s[way, at, k, row, :]
        return block.astype(jnp.int32).astype(jnp.float32) * jnp.concatenate([factor, factor], axis=1)

    def send_sum(way, slot, k, pieces, count):
        for piece, block in enumerate(pieces):
            most = jnp.max(jnp.abs(block), axis=0, keepdims=True)
            most = jnp.maximum(most[:, :128], most[:, 128:])
            factor = jnp.where(most > 0.0, 32767.0 / jnp.where(most > 0.0, most, 1.0), 0.0)
            factor = jnp.concatenate([factor, factor], axis=1)
            rows = pl.ds(piece * SCALE_ROWS, SCALE_ROWS)
            quant[way, slot, k, rows, :] = jnp.round(block * factor).astype(jnp.int32).astype(jnp.int16)
            at, row = scale_row(slot, piece)
            scale[way, at, k, row, :] = most * (1.0 / 32767.0)
        if count is not None:
            scale[way, slot // 2, k, pl.ds(7, 1), :] = count
        for copy in sum_copies(way, slot, k):
            copy.start()

    def take_u(unit):
        g, k = unit // CHUNKS, unit % CHUNKS

        @pl.when(g == 0)
        def _():
            for d in (0, 1, 3):
                ca_copy(k, d).wait_recv()
            c_copy(k).wait_recv()

        for place in range(PLACES):
            from_x, from_z = place % RING, place // RING
            tokens = jnp.concatenate([cols[k, 0, from_x, from_z], cols[k, 1, from_x, from_z]], axis=0)
            picked = jnp.dot(chosen[g, place], tokens, preferred_element_type=jnp.float32).astype(jnp.bfloat16)
            near[pl.ds(place * TAIL, TAIL), :] = picked[:TAIL]
            near[pl.ds(PLACES * TAIL + place * (PAIR - TAIL), PAIR - TAIL), :] = picked[TAIL:]
        part[...] = jnp.dot(wide[g], near[...], preferred_element_type=jnp.float32)

        def pieces(half):
            first = half * HALF
            return [part[first + SCALE_ROWS * piece:first + SCALE_ROWS * (piece + 1), :] for piece in range(2)]

        @pl.when(g == 0)
        def _():
            for way in (0, 1):
                send_sum(way, 0, k, pieces(way), hits[g])

        for way in (0, 1):
            @pl.when(g == 1 + way)
            def _():
                send_sum(way, 1, k, pieces(1 - way), None)
                kept[way, k] = part[way * HALF:(way + 1) * HALF, :]

        @pl.when(g == 3)
        def _():
            out_ref[:, pl.ds(pl.multiple_of(k * CHUNK, 128), CHUNK)] = part[...]

    def take_v(unit):
        k = unit % CHUNKS
        for way in (0, 1):
            @pl.when(unit // CHUNKS == way)
            def _():
                for copy in sum_copies(way, 0, k):
                    copy.wait_recv()
                pieces = [
                    kept[way, k, pl.ds(piece * SCALE_ROWS, SCALE_ROWS), :] + restored(way, 0, k, piece)
                    for piece in range(2)
                ]
                below = got_s[way, 0, k, pl.ds(7, 1), :]
                send_sum(way, 2, k, pieces, hits[1] + below if way == 0 else hits[2])

    actions = {
        "S": find_slots, "P": take_p, "XO": take_xo, "XA": take_xa, "XB": take_xb, "Z": send_z, "WZ": take_wz,
        "WZF": take_wzf, "C": take_c, "EXP": take_exp, "U": take_u, "V": take_v,
    }
    words, length = plan()

    def one_step(step, carry):
        code = looked_up(words, step)

        def among(names):
            if len(names) == 1:
                actions[names[0]](code - CODES[names[0]])
                return
            middle = len(names) // 2
            low = code < CODES[names[middle]]
            pl.when(low)(lambda: among(names[:middle]))
            pl.when(jnp.logical_not(low))(lambda: among(names[middle:]))

        among(list(CODES))
        return carry

    lax.fori_loop(0, length, one_step, 0)

    def drain(k, carry):
        for d in (1, 2, 3):
            z_copy(k, d).wait_send()
            for way in (0, 1):
                xa_copy(k, way, d).wait_send()
        for d in (0, 1, 3):
            ca_copy(k, d).wait_send()
        c_copy(k).wait_send()
        for way in (0, 1):
            xo_copy(k, way).wait_send()
            xb_copy(k, way).wait_send()
        return carry

    def drain_windows(g, carry):
        for d in (1, 2, 3):
            wx_copy(g, d).wait_send()
        for way in (0, 1):
            for d in range(RING):
                wz_copy(g, way, d).wait_send()
            for d in (2 * way, 2 * way + 1):
                wf_copy(g, way, d).wait_send()
        return carry

    for copy in pair_copies():
        copy.wait_send()
    lax.fori_loop(0, CHUNKS, drain, 0)
    lax.fori_loop(0, GROUPS, drain_windows, 0)

    def finish(place, carry):
        k = lax.shift_right_logical(jnp.int32(finish_word()), 4 * place) % 16
        for way in (0, 1):
            for slot in range(3):
                for copy in sum_copies(way, slot, k):
                    copy.wait_send()
        for way in (0, 1):
            for slot in (1, 2):
                for copy in sum_copies(way, slot, k):
                    copy.wait_recv()
        count = hits[3] + got_s[0, 1, k, pl.ds(7, 1), :] + got_s[1, 1, k, pl.ds(7, 1), :]
        inverse = 1.0 / jnp.sum(count, axis=1, keepdims=True)
        at = pl.ds(pl.multiple_of(k * CHUNK, 128), CHUNK)
        for half in (0, 1):
            for piece in (0, 1):
                rows = pl.ds(half * HALF + piece * SCALE_ROWS, SCALE_ROWS)
                total = out_ref[rows, at] + restored(half, 2, k, piece) + restored(1 - half, 1, k, piece)
                out_ref[rows, at] = total * inverse
        return carry

    lax.fori_loop(0, CHUNKS, finish, 0)


def shards(tokens, routes, slab_start):
    dma = pltpu.SemaphoreType.DMA
    bf16, f32, i16 = jnp.bfloat16, jnp.float32, jnp.int16
    result = pl.pallas_call(
        gram_kernel,
        out_shape=pltpu.VMEM((SLAB, BLOCK), f32),
        in_specs=[
            pl.BlockSpec(memory_space=pltpu.SMEM),
            pl.BlockSpec(memory_space=pltpu.VMEM),
            pl.BlockSpec(memory_space=pl.ANY),
        ],
        out_specs=pl.BlockSpec(memory_space=pltpu.VMEM),
        scratch_shapes=[
            pltpu.VMEM((2 * TOK, WIDTH), bf16),
            pltpu.VMEM((2, 8, TOK), jnp.int32),
            pltpu.VMEM((GROUPS * RING, 2 * TOK), f32),
            pltpu.VMEM((GROUPS * RING, FULL + TAIL, 128), bf16),
            pltpu.VMEM((GROUPS, RING, RING, FULL + TAIL, 128), bf16),
            pltpu.VMEM((GROUPS, PLACES, PAIR, 2 * TOK), bf16),
            pltpu.VMEM((GROUPS, SLAB, PLACES * PAIR), bf16),
            pltpu.VMEM((CHUNKS, 2, RING, RING, TOK, CHUNK), bf16),
            pltpu.VMEM((PLACES * PAIR, CHUNK), bf16),
            pltpu.VMEM((SLAB, CHUNK), f32),
            pltpu.VMEM((2, CHUNKS, HALF, CHUNK), f32),
            pltpu.VMEM((2, 3, CHUNKS, HALF, CHUNK), i16),
            pltpu.VMEM((2, 2, CHUNKS, 8, 128), f32),
            pltpu.VMEM((2, 3, CHUNKS, HALF, CHUNK), i16),
            pltpu.VMEM((2, 2, CHUNKS, 8, 128), f32),
            pltpu.VMEM((GROUPS, 1, TOK), f32),
            dma((2,)), dma((2,)), dma(()),
            dma((CHUNKS, 3)), dma((CHUNKS, 3)), dma((CHUNKS,)),
            dma((CHUNKS, 2)), dma((CHUNKS, 2)), dma((CHUNKS, 2, 3)), dma((CHUNKS, 2, 3)), dma((CHUNKS, 2)), dma((CHUNKS, 2)),
            dma((CHUNKS, 4)), dma((CHUNKS, 4)), dma((CHUNKS,)), dma((CHUNKS,)),
            dma((GROUPS, 3)), dma((GROUPS, 3)), dma((GROUPS, 2, RING)), dma((GROUPS, 2, RING)), dma((GROUPS, 2, 2)), dma((GROUPS, 2, 2)),
            dma((2, 3, CHUNKS)), dma((2, 3, CHUNKS)), dma((2, 2, CHUNKS)), dma((2, 2, CHUNKS)),
        ],
        compiler_params=pltpu.CompilerParams(
            collective_id=0, has_side_effects=True, vmem_limit_bytes=56 * 2**20
        ),
        name="gram",
    )(slab_start, routes.T, tokens)
    return result[None]


def solution(mesh):
    placed = (P(("expert", "dp"), None), P(("expert", "dp"), None), P())
    return jax.shard_map(
        shards, mesh=mesh, in_specs=placed, out_specs=P("expert", None, "dp"), check_vma=False
    )
```

```python
import jax
import jax.numpy as jnp
from jax import lax
from jax.experimental import pallas as pl
from jax.experimental.pallas import tpu as pltpu
from jax.sharding import PartitionSpec as P

MESH = pl.DeviceIdType.MESH
SLAB = 448
CAP = 40
PAIR = 2 * CAP
FULL = 3 * PAIR
TAIL = 48
RING = 4
TOK = 128
WIDTH = 7168
BLOCK = WIDTH // RING
CHUNK = 256
CHUNKS = BLOCK // CHUNK
PLACES = RING * RING
GROUPS = 4
OFFSETS = (2, 1, 3, 0)
SCALE_ROWS = 112
HALF = SLAB // 2
SPAN = 640

CODES = {
    "U": 0, "V": 28, "XO": 42, "XA": 49, "XB": 56, "C": 63, "Z": 70, "P": 77, "WZ": 81, "WZF": 85, "EXP": 89, "S": 93,
}
SCHEDULE = (
    "XO1", "XO0", "XO4", "Z4", "XA0", "S0", "P0", "P1", "XA1", "P2", "WZ0", "XB0", "XA4", "WZ1", "WZF0", "C0",
    "WZ2", "WZF1", "XB1", "EXP0", "XB4", "XO2", "XA2", "XO6", "U00", "C1", "WZF2", "P3", "C4", "U01", "EXP1", "U10",
    "U04", "EXP2", "Z5", "U21", "XB2", "V00", "XO5", "U20", "Z6", "V11", "U14", "XA5", "U24", "V04", "C2", "U11",
    "XA6", "V01", "Z3", "WZ3", "V10", "U02", "XB5", "V14", "U22", "U12", "XB6", "XO3", "V12", "C5", "XA3", "WZF3",
    "V02", "U05", "C6", "U15", "U25", "EXP3", "U06", "XB3", "V15", "U36", "V05", "U16", "U26", "C3", "V06", "U32",
    "V16", "U30", "U03", "U23", "U13", "U35", "U33", "U34", "V03", "V13", "U31",
)


def plan():
    codes = []
    for item in SCHEDULE:
        name = item.rstrip("0123456789")
        digits = item[len(name):]
        value = int(digits[0]) * CHUNKS + int(digits[1]) if len(digits) == 2 else int(digits)
        codes.append(CODES[name] + value)
    padded = codes + [0] * (-len(codes) % 4)
    words = [sum(padded[at + i] * 128 ** i for i in range(4)) for at in range(0, len(padded), 4)]
    return words, len(codes)


def finish_word():
    last = {}
    for at, item in enumerate(SCHEDULE):
        if item[0] == "V" or item[:2] in ("U1", "U2"):
            last[int(item[2])] = at
    return sum(k * 16 ** place for place, k in enumerate(sorted(last, key=last.get)))


def looked_up(words, step):
    word = jnp.int32(words[0])
    for at in range(1, len(words)):
        word = jnp.where(step // 4 == at, jnp.int32(words[at]), word)
    return lax.shift_right_logical(word, 7 * (step % 4)) % 128


def offset_of(group):
    value = jnp.int32(OFFSETS[0])
    for index in range(1, GROUPS):
        value = jnp.where(group == index, jnp.int32(OFFSETS[index]), value)
    return value


def gram_kernel(
    start_ref, routes_ref, tok_ref, out_ref,
    both, listed, slots, packed, win, chosen, wide, cols, near, part, kept, quant, scale, got_q, got_s, hits,
    pair_s, pair_r, own_s, z_s, z_r, zl_s, xo_s, xo_r, xa_s, xa_r, xb_s, xb_r, ca_s, ca_r, c_s, c_r,
    wx_s, wx_r, wz_s, wz_r, wf_s, wf_r, q_s, q_r, f_s, f_r,
):
    expert = lax.axis_index("expert")
    z = lax.axis_index("dp")
    core = expert % 2
    x = (expert // 2) % RING
    y = expert // (2 * RING)

    def device(dy=0, dx=0, dz=0, dc=0):
        ey, ex, ec = (y + dy) % RING, (x + dx) % RING, (core + dc) % 2
        return ((ey * RING + ex) * 2 + ec, (z + dz) % RING)

    def remote(src, dst, send, recv, to):
        return pltpu.make_async_remote_copy(
            src_ref=src, dst_ref=dst, send_sem=send, recv_sem=recv, device_id=to, device_id_type=MESH
        )

    def pair_copies():
        return (
            remote(routes_ref, listed.at[core], pair_s.at[0], pair_r.at[0], device(dc=1)),
            remote(tok_ref, both.at[pl.ds(core * TOK, TOK)], pair_s.at[1], pair_r.at[1], device(dc=1)),
        )

    def own_copy():
        return pltpu.make_async_copy(tok_ref, both.at[pl.ds(core * TOK, TOK)], own_s)

    def z_copy(k, d):
        first = pl.multiple_of(((z + d) % RING) * BLOCK + k * CHUNK, 128)
        return remote(
            tok_ref.at[:, pl.ds(first, CHUNK)], cols.at[k, core, x, z], z_s.at[k, d - 1], z_r.at[k, d - 1], device(dz=d)
        )

    def z_local(k):
        first = pl.multiple_of(z * BLOCK + k * CHUNK, 128)
        return pltpu.make_async_copy(tok_ref.at[:, pl.ds(first, CHUNK)], cols.at[k, core, x, z], zl_s.at[k])

    def xo_copy(k, way):
        here = cols.at[k, core, x, z]
        return remote(here, here, xo_s.at[k, way], xo_r.at[k, way], device(dx=1 if way == 0 else 3))

    def xa_copy(k, way, d):
        here = cols.at[k, core, x, (z + RING - d) % RING]
        return remote(here, here, xa_s.at[k, way, d - 1], xa_r.at[k, way, d - 1], device(dx=1 if way == 0 else 3))

    def xb_copy(k, way):
        origin = (x + (3 if way == 0 else 1)) % RING
        here = cols.at[k, core, origin, pl.ds(2 * way, 2)]
        return remote(here, here, xb_s.at[k, way], xb_r.at[k, way], device(dx=1 if way == 0 else 3))

    def ca_copy(k, d):
        here = cols.at[k, core, (x + d) % RING]
        return remote(here, here, ca_s.at[k, d % RING], ca_r.at[k, d % RING], device(dc=1))

    def c_copy(k):
        here = cols.at[k, core, (x + 2) % RING]
        return remote(here, here, c_s.at[k], c_r.at[k], device(dc=1))

    def wx_copy(g, d):
        return remote(
            packed.at[g * RING + d], win.at[g, z, x], wx_s.at[g, d - 1], wx_r.at[g, d - 1], device(dx=d)
        )

    def wz_copy(g, way, d):
        here = win.at[g, z, (x + RING - d) % RING]
        return remote(here, here, wz_s.at[g, way, d], wz_r.at[g, way, d], device(dz=1 if way == 0 else 3))

    def wf_copy(g, way, d):
        here = win.at[g, (z + (3 if way == 0 else 1)) % RING, (x + RING - d) % RING]
        return remote(here, here, wf_s.at[g, way, d % 2], wf_r.at[g, way, d % 2], device(dz=1 if way == 0 else 3))

    def sum_copies(way, slot, k):
        to = device(dy=1 if way == 0 else 3)
        values = remote(quant.at[way, slot, k], got_q.at[way, slot, k], q_s.at[way, slot, k], q_r.at[way, slot, k], to)
        if slot == 1:
            return (values,)
        at = slot // 2
        return (values, remote(scale.at[way, at, k], got_s.at[way, at, k], f_s.at[way, at, k], f_r.at[way, at, k], to))

    for k in range(CHUNKS):
        z_local(k).start()
    own_copy().start()

    barrier = pltpu.get_barrier_semaphore()
    peers = [device(dc=1), device(dy=1), device(dy=3)]
    peers += [device(dx=d) for d in (1, 2, 3)] + [device(dz=d) for d in (1, 2, 3)]
    for peer in peers:
        pl.semaphore_signal(barrier, inc=1, device_id=peer, device_id_type=MESH)
    pl.semaphore_wait(barrier, len(peers))

    def send_z(k):
        for d in (1, 3, 2):
            z_copy(k, d).start()

    send_z(jnp.int32(0))
    for copy in pair_copies():
        copy.start()
    for k in (1, 2):
        send_z(jnp.int32(k))
    listed[core] = routes_ref[...]

    def take_xo(k):
        z_local(k).wait()
        for way in (0, 1):
            xo_copy(k, way).start()

    def take_xa(k):
        for d in (1, 3, 2):
            z_copy(k, d).wait_recv()
            for way in (0, 1):
                xa_copy(k, way, d).start()

    def take_xb(k):
        for way in (0, 1):
            xo_copy(k, way).wait_recv()
            for d in (1, 2, 3):
                xa_copy(k, way, d).wait_recv()
            xb_copy(k, way).start()
        for d in (0, 1, 3):
            ca_copy(k, d).start()

    def take_c(k):
        for way in (0, 1):
            xb_copy(k, way).wait_recv()
        c_copy(k).start()

    def find_slots(_):
        for copy in pair_copies():
            copy.wait_recv()
        own_copy().wait()
        named = jnp.concatenate([listed[0], listed[1]], axis=1)
        row = lax.broadcasted_iota(jnp.int32, (GROUPS * RING, 2 * TOK), 0)
        group, step = row // RING, row % RING
        away = jnp.where(group == 0, OFFSETS[0], jnp.where(group == 1, OFFSETS[1], jnp.where(group == 2, OFFSETS[2], OFFSETS[3])))
        label = (((y + away) % RING) * RING + (x + step) % RING) * 2 + core
        hit = jnp.zeros((GROUPS * RING, 2 * TOK), jnp.float32)
        for choice in range(named.shape[0]):
            hit += jnp.where(named[choice:choice + 1, :] == label, 1.0, 0.0)
        before = lax.broadcasted_iota(jnp.int32, (2 * TOK, 2 * TOK), 0) < lax.broadcasted_iota(
            jnp.int32, (2 * TOK, 2 * TOK), 1
        )
        rank = jnp.dot(
            hit.astype(jnp.bfloat16), jnp.where(before, 1.0, 0.0).astype(jnp.bfloat16), preferred_element_type=jnp.float32
        )
        slots[...] = jnp.where(hit > 0.0, rank, -1.0)

    def take_p(g):
        slot = lax.broadcasted_iota(jnp.int32, (PAIR, 2 * TOK), 0).astype(jnp.float32)
        source = lax.broadcasted_iota(jnp.int32, (SPAN, SLAB), 0)
        target = lax.broadcasted_iota(jnp.int32, (SPAN, SLAB), 1)
        for d in (2, 1, 3, 0):
            row = g * RING + d
            taken = jnp.where(slots[pl.ds(row, 1), :] == slot, 1.0, 0.0).astype(jnp.bfloat16)
            label = (((y + offset_of(g)) % RING) * RING + (x + d) % RING) * 2 + core
            start = start_ref[label]
            tile = jnp.minimum(lax.div(start, jnp.int32(128)), (WIDTH - SPAN) // 128)
            shift = start - tile * 128
            first = tile * 128
            rows = both[:, pl.ds(first, SPAN)]
            picked = jnp.dot(taken, rows, preferred_element_type=jnp.float32)
            moved = jnp.where(source == target + shift, 1.0, 0.0).astype(jnp.bfloat16)
            picked = jnp.dot(picked.astype(jnp.bfloat16), moved, preferred_element_type=jnp.float32)
            rest = picked[:, 384:SLAB]
            seat = slots[pl.ds(row, 1), :]
            seats = [seat[:, 64 * part:64 * part + 64] for part in range(4)] + [jnp.zeros((12, 64), jnp.float32)]
            tail = jnp.concatenate([rest[:TAIL], jnp.concatenate([rest[TAIL:]] + seats, axis=0)], axis=1)
            blocks = [picked[:, 128 * tile:128 * tile + 128] for tile in range(3)] + [tail]
            value = jnp.concatenate(blocks, axis=0).astype(jnp.bfloat16)
            if d == 0:
                win[g, z, x] = value
                for way in (0, 1):
                    wz_copy(g, way, 0).start()
            else:
                packed[row] = value
                wx_copy(g, d).start()

    def take_wz(g):
        for d in (1, 3, 2):
            wx_copy(g, d).wait_recv()
            for way in (0, 1):
                wz_copy(g, way, d).start()

    def take_wzf(g):
        for way in (0, 1):
            for d in (2 * way, 2 * way + 1):
                wz_copy(g, way, d).wait_recv()
                wf_copy(g, way, d).start()

    def take_exp(g):
        for way in (0, 1):
            for d in (2 * way, 2 * way + 1):
                wz_copy(g, 1 - way, d).wait_recv()
                wf_copy(g, way, d).wait_recv()
        slot = lax.broadcasted_iota(jnp.int32, (PAIR, 2 * TOK), 0).astype(jnp.float32)
        low = lax.broadcasted_iota(jnp.int32, (1, 128), 1) < 64
        total = jnp.zeros((1, 2 * TOK), jnp.float32)
        seats = win[g, :, :, FULL + PAIR - TAIL:, :].reshape(PLACES * 16, 128).astype(jnp.float32)[:, 64:]
        seats = jnp.concatenate([seats, seats], axis=1)
        for place in range(PLACES):
            rows = [seats[16 * place + part:16 * place + part + 1] for part in range(4)]
            seat = jnp.concatenate([jnp.where(low, rows[0], rows[1]), jnp.where(low, rows[2], rows[3])], axis=1)
            chosen[g, place] = jnp.where(seat == slot, 1.0, 0.0).astype(jnp.bfloat16)
            total += jnp.where(seat >= 0.0, 1.0, 0.0)
        hits[g] = total[:, :TOK] + total[:, TOK:]
        split = PLACES * TAIL
        for tile in range(3):
            at = tile * PAIR
            block = win[g, :, :, at:at + TAIL, :].reshape(split, 128)
            wide[g, tile * 128:(tile + 1) * 128, :split] = block.T
            block = win[g, :, :, at + TAIL:at + PAIR, :].reshape(PLACES * (PAIR - TAIL), 128)
            wide[g, tile * 128:(tile + 1) * 128, split:] = block.T
        wide[g, 384:, :split] = win[g, :, :, FULL:, :].reshape(split, 128).T[:64]
        wide[g, 384:, split:] = win[g, :, :, FULL:FULL + PAIR - TAIL, :].reshape(PLACES * (PAIR - TAIL), 128).T[64:]

    def scale_row(slot, piece):
        return (slot + 1) // 2, pl.ds(piece + (2 if slot == 1 else 0), 1)

    def restored(way, slot, k, piece):
        block = got_q[way, slot, k, pl.ds(piece * SCALE_ROWS, SCALE_ROWS), :]
        at, row = scale_row(slot, piece)
        factor = got_s[way, at, k, row, :]
        return block.astype(jnp.int32).astype(jnp.float32) * jnp.concatenate([factor, factor], axis=1)

    def send_sum(way, slot, k, pieces, count):
        for piece, block in enumerate(pieces):
            most = jnp.max(jnp.abs(block), axis=0, keepdims=True)
            most = jnp.maximum(most[:, :128], most[:, 128:])
            factor = jnp.where(most > 0.0, 32767.0 / jnp.where(most > 0.0, most, 1.0), 0.0)
            factor = jnp.concatenate([factor, factor], axis=1)
            rows = pl.ds(piece * SCALE_ROWS, SCALE_ROWS)
            quant[way, slot, k, rows, :] = jnp.round(block * factor).astype(jnp.int32).astype(jnp.int16)
            at, row = scale_row(slot, piece)
            scale[way, at, k, row, :] = most * (1.0 / 32767.0)
        if count is not None:
            scale[way, slot // 2, k, pl.ds(7, 1), :] = count
        for copy in sum_copies(way, slot, k):
            copy.start()

    def take_u(unit):
        g, k = unit // CHUNKS, unit % CHUNKS

        @pl.when(g == 0)
        def _():
            for d in (0, 1, 3):
                ca_copy(k, d).wait_recv()
            c_copy(k).wait_recv()

        for place in range(PLACES):
            from_x, from_z = place % RING, place // RING
            tokens = jnp.concatenate([cols[k, 0, from_x, from_z], cols[k, 1, from_x, from_z]], axis=0)
            picked = jnp.dot(chosen[g, place], tokens, preferred_element_type=jnp.float32).astype(jnp.bfloat16)
            near[pl.ds(place * TAIL, TAIL), :] = picked[:TAIL]
            near[pl.ds(PLACES * TAIL + place * (PAIR - TAIL), PAIR - TAIL), :] = picked[TAIL:]
        part[...] = jnp.dot(wide[g], near[...], preferred_element_type=jnp.float32)

        def pieces(half):
            first = half * HALF
            return [part[first + SCALE_ROWS * piece:first + SCALE_ROWS * (piece + 1), :] for piece in range(2)]

        @pl.when(g == 0)
        def _():
            for way in (0, 1):
                send_sum(way, 0, k, pieces(way), hits[g])

        for way in (0, 1):
            @pl.when(g == 1 + way)
            def _():
                send_sum(way, 1, k, pieces(1 - way), None)
                kept[way, k] = part[way * HALF:(way + 1) * HALF, :]

        @pl.when(g == 3)
        def _():
            out_ref[:, pl.ds(pl.multiple_of(k * CHUNK, 128), CHUNK)] = part[...]

    def take_v(unit):
        k = unit % CHUNKS
        for way in (0, 1):
            @pl.when(unit // CHUNKS == way)
            def _():
                for copy in sum_copies(way, 0, k):
                    copy.wait_recv()
                pieces = [
                    kept[way, k, pl.ds(piece * SCALE_ROWS, SCALE_ROWS), :] + restored(way, 0, k, piece)
                    for piece in range(2)
                ]
                below = got_s[way, 0, k, pl.ds(7, 1), :]
                send_sum(way, 2, k, pieces, hits[1] + below if way == 0 else hits[2])

    actions = {
        "S": find_slots, "P": take_p, "XO": take_xo, "XA": take_xa, "XB": take_xb, "Z": send_z, "WZ": take_wz,
        "WZF": take_wzf, "C": take_c, "EXP": take_exp, "U": take_u, "V": take_v,
    }
    words, length = plan()

    def one_step(step, carry):
        code = looked_up(words, step)

        def among(names):
            if len(names) == 1:
                actions[names[0]](code - CODES[names[0]])
                return
            middle = len(names) // 2
            low = code < CODES[names[middle]]
            pl.when(low)(lambda: among(names[:middle]))
            pl.when(jnp.logical_not(low))(lambda: among(names[middle:]))

        among(list(CODES))
        return carry

    lax.fori_loop(0, length, one_step, 0)

    def drain(k, carry):
        for d in (1, 2, 3):
            z_copy(k, d).wait_send()
            for way in (0, 1):
                xa_copy(k, way, d).wait_send()
        for d in (0, 1, 3):
            ca_copy(k, d).wait_send()
        c_copy(k).wait_send()
        for way in (0, 1):
            xo_copy(k, way).wait_send()
            xb_copy(k, way).wait_send()
        return carry

    def drain_windows(g, carry):
        for d in (1, 2, 3):
            wx_copy(g, d).wait_send()
        for way in (0, 1):
            for d in range(RING):
                wz_copy(g, way, d).wait_send()
            for d in (2 * way, 2 * way + 1):
                wf_copy(g, way, d).wait_send()
        return carry

    for copy in pair_copies():
        copy.wait_send()
    lax.fori_loop(0, CHUNKS, drain, 0)
    lax.fori_loop(0, GROUPS, drain_windows, 0)

    def finish(place, carry):
        k = lax.shift_right_logical(jnp.int32(finish_word()), 4 * place) % 16
        for way in (0, 1):
            for slot in range(3):
                for copy in sum_copies(way, slot, k):
                    copy.wait_send()
        for way in (0, 1):
            for slot in (1, 2):
                for copy in sum_copies(way, slot, k):
                    copy.wait_recv()
        count = hits[3] + got_s[0, 1, k, pl.ds(7, 1), :] + got_s[1, 1, k, pl.ds(7, 1), :]
        inverse = 1.0 / jnp.sum(count, axis=1, keepdims=True)
        at = pl.ds(pl.multiple_of(k * CHUNK, 128), CHUNK)
        for half in (0, 1):
            for piece in (0, 1):
                rows = pl.ds(half * HALF + piece * SCALE_ROWS, SCALE_ROWS)
                total = out_ref[rows, at] + restored(half, 2, k, piece) + restored(1 - half, 1, k, piece)
                out_ref[rows, at] = total * inverse
        return carry

    lax.fori_loop(0, CHUNKS, finish, 0)


def shards(tokens, routes, slab_start):
    dma = pltpu.SemaphoreType.DMA
    bf16, f32, i16 = jnp.bfloat16, jnp.float32, jnp.int16
    result = pl.pallas_call(
        gram_kernel,
        out_shape=pltpu.VMEM((SLAB, BLOCK), f32),
        in_specs=[
            pl.BlockSpec(memory_space=pltpu.SMEM),
            pl.BlockSpec(memory_space=pltpu.VMEM),
            pl.BlockSpec(memory_space=pl.ANY),
        ],
        out_specs=pl.BlockSpec(memory_space=pltpu.VMEM),
        scratch_shapes=[
            pltpu.VMEM((2 * TOK, WIDTH), bf16),
            pltpu.VMEM((2, 8, TOK), jnp.int32),
            pltpu.VMEM((GROUPS * RING, 2 * TOK), f32),
            pltpu.VMEM((GROUPS * RING, FULL + TAIL, 128), bf16),
            pltpu.VMEM((GROUPS, RING, RING, FULL + TAIL, 128), bf16),
            pltpu.VMEM((GROUPS, PLACES, PAIR, 2 * TOK), bf16),
            pltpu.VMEM((GROUPS, SLAB, PLACES * PAIR), bf16),
            pltpu.VMEM((CHUNKS, 2, RING, RING, TOK, CHUNK), bf16),
            pltpu.VMEM((PLACES * PAIR, CHUNK), bf16),
            pltpu.VMEM((SLAB, CHUNK), f32),
            pltpu.VMEM((2, CHUNKS, HALF, CHUNK), f32),
            pltpu.VMEM((2, 3, CHUNKS, HALF, CHUNK), i16),
            pltpu.VMEM((2, 2, CHUNKS, 8, 128), f32),
            pltpu.VMEM((2, 3, CHUNKS, HALF, CHUNK), i16),
            pltpu.VMEM((2, 2, CHUNKS, 8, 128), f32),
            pltpu.VMEM((GROUPS, 1, TOK), f32),
            dma((2,)), dma((2,)), dma(()),
            dma((CHUNKS, 3)), dma((CHUNKS, 3)), dma((CHUNKS,)),
            dma((CHUNKS, 2)), dma((CHUNKS, 2)), dma((CHUNKS, 2, 3)), dma((CHUNKS, 2, 3)), dma((CHUNKS, 2)), dma((CHUNKS, 2)),
            dma((CHUNKS, 4)), dma((CHUNKS, 4)), dma((CHUNKS,)), dma((CHUNKS,)),
            dma((GROUPS, 3)), dma((GROUPS, 3)), dma((GROUPS, 2, RING)), dma((GROUPS, 2, RING)), dma((GROUPS, 2, 2)), dma((GROUPS, 2, 2)),
            dma((2, 3, CHUNKS)), dma((2, 3, CHUNKS)), dma((2, 2, CHUNKS)), dma((2, 2, CHUNKS)),
        ],
        compiler_params=pltpu.CompilerParams(
            collective_id=0, has_side_effects=True, vmem_limit_bytes=56 * 2**20
        ),
        name="gram",
    )(slab_start, routes.T, tokens)
    return result[None]


def solution(mesh):
    placed = (P(("expert", "dp"), None), P(("expert", "dp"), None), P())
    return jax.shard_map(
        shards, mesh=mesh, in_specs=placed, out_specs=P("expert", None, "dp"), check_vma=False
    )
```
